128 devices in a mesh: segment: 2 (over y_hi), expert: 64 (over z, y_lo, x, core).
Axes of the slice: x: 4, y: 4 (y_hi: 2, y_lo: 2; y = y_hi * 2 + y_lo), z: 4, core: 2. Of those that a mesh axis runs over, the one named last changes fastest.
Arguments:
- forward_inputs: bfloat16 [2, 8192, 2048], P('segment', 'expert'), may hold values from -6 to 6
- backward_inputs: bfloat16 [2, 8192, 2048], P('segment', 'expert'), may hold values from -6 to 6
- backward_cotangents: bfloat16 [2, 8192, 2048], P('segment', 'expert'), may hold values from -6 to 6
- routes: int32 [2, 2, 8192, 8], P(None, 'segment', 'expert'), may hold values from 0 to 63, all different within a row; in each aligned block of 128 rows (0 to 127, 128 to 255, ..., all dimensions but the last counted through in order) at most 17 rows name the same one
- route_weights: float32 [2, 2, 8192, 8], P(None, 'segment', 'expert'), may hold values from 0.05 to 0.5
- w_gate: bfloat16 [2, 64, 2048, 768], P('segment', 'expert'), may hold values from -0.125 to 0.125
- w_up: bfloat16 [2, 64, 2048, 768], P('segment', 'expert'), may hold values from -0.125 to 0.125
- w_down: bfloat16 [2, 64, 768, 2048], P('segment', 'expert'), may hold values from -0.21875 to 0.21875
Outputs:
- finished: bfloat16 [2, 8192, 2048], P('segment', 'expert')
- handed: bfloat16 [2, 8192, 2048], P('segment', 'expert')
The draws below stay inside these ranges and needn't reach their ends.
Inputs may be any that keep to these rules, and one draw needn't show every extreme that they name: `routes`: within the rows of one device (aligned blocks of 128 tokens, for each pass and section) no expert is named by more than 17 (token, pick) pairs, a bound that some block reaches; the 8 experts of a token differ.
All inputs are finite; a program needn't handle non-finite values.
Results may differ from the reference program's by a relative error of at most 0.0047.
Values may be sent and summed in bfloat16 or wider, within the bound.
A program may use at most 128 MiB of HBM per device.

```python
import math
import jax
import jax.numpy as jnp
import numpy as np
from jax import lax

D = 2048
FF = 768
TOP = 8
TOK_DEV = 128
EXPERTS = 64
TOKENS = 8192
CAP = 17


def levels(rng, shape, pieces, low, high):
    gain, own = 1.0, jax.random.fold_in(rng, 6)
    for position, parts in pieces:
        heights = jnp.exp(jax.random.uniform(jax.random.fold_in(own, position), (parts,), jnp.float32, low / len(pieces), high / len(pieces)))
        gain = gain * jnp.repeat(heights, shape[position] // parts).reshape([-1 if axis == position else 1 for axis in range(len(shape))])
    return gain


def shared_out(stream_key, own, number, rows, amount, top, limit, skew):
    ranking = jax.random.permutation(stream_key, amount)
    heavy_load, ordinary = portions_of(amount, rows * top, limit, skew, True), portions_of(amount, rows * top, limit, skew, False)
    places = jnp.arange(amount)

    def named(sizes, rotation):
        used = int((sizes > 0).sum())
        fixed = max(1, used // 4)
        passed = fixed + (places - fixed + rotation * (used - fixed)) % max(1, amount - fixed)
        return jnp.zeros((amount,), jnp.int32).at[ranking[jnp.where(places < fixed, places, passed)]].set(jnp.asarray(sizes, jnp.int32))

    sizes = jnp.where(number % 4 == 0, named(heavy_load, number // 4), named(ordinary, number - number // 4 - 1))
    mixed = jax.random.permutation(jax.random.fold_in(own, 3), amount)
    source_of, receiver = mixed[0:amount // 2 * 2:2], mixed[1:amount // 2 * 2:2]
    room = jnp.minimum(sizes[source_of] - 1, limit - sizes[receiver]) // 2
    room = jnp.where((source_of == ranking[0]) | (receiver == ranking[0]) | (sizes[receiver] == 0), 0, jnp.maximum(room, 0))
    passed = jax.random.randint(jax.random.fold_in(own, 4), (amount // 2,), 0, 1 << 20) % (room + 1)
    sizes = sizes.at[source_of].add(-passed).at[receiver].add(passed)
    members = jnp.searchsorted(jnp.cumsum(sizes), jnp.arange(rows * top), side="right").astype(jnp.int32)
    grid = members.reshape(top, rows).T
    grid = grid[jax.random.permutation(jax.random.fold_in(own, 1), rows)]
    rotation = jax.random.randint(jax.random.fold_in(own, 2), (rows, 1), 0, top)
    return jnp.take_along_axis(grid, (jnp.arange(top)[None, :] + rotation) % top, axis=1)


def portions_of(number_of, total, limit, slope, full):
    loads = [(1 << 20) // math.isqrt(rank ** slope) + 1 for rank in range(1, number_of + 1)]
    largest = limit if full else min(limit, max(-(-total // number_of), total * loads[0] // sum(loads)))
    least = 1 if total - largest >= number_of - 1 else 0
    holding, surplus = [largest] + [least] * (number_of - 1), total - largest - least * (number_of - 1)
    while surplus > 0:
        movable = [i for i in range(1, number_of) if holding[i] < largest] or [i for i in range(1, number_of) if holding[i] < limit]
        mass, budget = sum([loads[i] for i in movable]), surplus
        for i in movable:
            addition = min(limit - holding[i], max(1, budget * loads[i] // mass), surplus)
            holding[i] = holding[i] + addition
            surplus = surplus - addition
    return np.array(holding)


def noise(rng, dims, scale, bound, cuts=(), kind=jnp.bfloat16):
    level = levels(rng, dims, cuts, -0.22, 0.18) if cuts else 1.0
    result = jax.random.normal(rng, dims, jnp.float32) * scale * level
    return jnp.minimum(jnp.maximum(result, -bound), bound).astype(kind)


def setup_inputs(seed: int = 0) -> dict:
    key_list = jax.random.split(jax.random.key(seed), 9)
    forward_inputs = noise(key_list[0], (2, TOKENS, D), 1.0, 6.0, ((0, 2), (1, 64)))
    backward_inputs = noise(key_list[1], (2, TOKENS, D), 1.0, 6.0, ((0, 2), (1, 64)))
    backward_cotangents = noise(key_list[2], (2, TOKENS, D), 1.0, 6.0, ((0, 2), (1, 64)))
    routes_keys = jax.random.split(jax.random.fold_in(key_list[3], 1), 2 * 2 * TOKENS // TOK_DEV)
    routes_turns = jax.random.permutation(jax.random.fold_in(key_list[3], 3), 2 * 2 * TOKENS // TOK_DEV)
    routes = jax.vmap(lambda own, number: shared_out(jax.random.fold_in(key_list[3], 2), own, number, TOK_DEV, EXPERTS, TOP, CAP, 1))(routes_keys, routes_turns).reshape((2, 2, TOKENS, TOP))
    route_weights = jnp.clip(jnp.exp(math.log(0.5) - 2.3025851 * jax.random.uniform(key_list[4], (2, 2, TOKENS, TOP), jnp.float32) ** levels(key_list[4], (2, 2, TOKENS, TOP), ((1, 2), (2, 64)), -0.2, 0.2)), 0.05, 0.5)
    w_gate = noise(key_list[5], (2, EXPERTS, D, FF), D ** -0.5, 0.125, ((0, 2), (1, 64)))
    w_up = noise(key_list[6], (2, EXPERTS, D, FF), D ** -0.5, 0.125, ((0, 2), (1, 64)))
    w_down = noise(key_list[7], (2, EXPERTS, FF, D), FF ** -0.5, 0.21875, ((0, 2), (1, 64)))
    return {"forward_inputs": forward_inputs, "backward_inputs": backward_inputs, "backward_cotangents": backward_cotangents, "routes": routes, "route_weights": route_weights, "w_gate": w_gate, "w_up": w_up, "w_down": w_down}


def dot_transposed(left, right):
    return lax.dot_general(left, right, (((1,), (1,)), ((), ())), preferred_element_type=jnp.float32)


def slot_plan(route_block, expert_count, capacity):
    flat_routes = route_block.reshape(-1).astype(jnp.int32)
    onehot = (flat_routes[:, None] == jnp.arange(expert_count, dtype=jnp.int32)[None, :]).astype(jnp.int32)
    placed = jnp.sum((jnp.cumsum(onehot, axis=0) - 1) * onehot, axis=1)
    targets = flat_routes * capacity + placed
    pair_index = jnp.arange(flat_routes.shape[0], dtype=jnp.int32)
    source_row = jnp.zeros((expert_count * capacity,), jnp.int32).at[targets].set(pair_index // route_block.shape[1])
    filled = jnp.zeros((expert_count * capacity,), jnp.int32).at[targets].set(1)
    return targets, source_row, filled


def pack_rows(row_block, source_row, filled):
    return jnp.where(filled[:, None] > 0, row_block[source_row], jnp.zeros((), row_block.dtype))


def gate_combine(results, targets, weight_block):
    picked = results[targets].reshape(weight_block.shape[0], weight_block.shape[1], results.shape[1])
    return jnp.einsum("tj,tjd->td", weight_block.astype(jnp.float32), picked.astype(jnp.float32))


def expert_forward(row_block, gate_w, up_w, down_w):
    gate_pre = jnp.dot(row_block, gate_w, preferred_element_type=jnp.float32)
    up_pre = jnp.dot(row_block, up_w, preferred_element_type=jnp.float32)
    hidden = (jax.nn.silu(gate_pre) * up_pre).astype(jnp.bfloat16)
    return jnp.dot(hidden, down_w, preferred_element_type=jnp.float32).astype(jnp.bfloat16)


def expert_backward(row_block, cotangent, gate_w, up_w, down_w):
    gate_pre = jnp.dot(row_block, gate_w, preferred_element_type=jnp.float32)
    up_pre = jnp.dot(row_block, up_w, preferred_element_type=jnp.float32)
    back_hidden = dot_transposed(cotangent, down_w)
    sigmoid_gate = jax.nn.sigmoid(gate_pre)
    d_gate = (back_hidden * up_pre * sigmoid_gate * (1.0 + gate_pre * (1.0 - sigmoid_gate))).astype(jnp.bfloat16)
    d_up = (back_hidden * gate_pre * sigmoid_gate).astype(jnp.bfloat16)
    return (dot_transposed(d_gate, gate_w) + dot_transposed(d_up, up_w)).astype(jnp.bfloat16)


def to_experts(packed, block_count):
    width = packed.shape[-1]
    return packed.reshape(block_count, EXPERTS, CAP, width).transpose(1, 0, 2, 3).reshape(EXPERTS, block_count * CAP, width)


def from_experts(results, block_count):
    width = results.shape[-1]
    return results.reshape(EXPERTS, block_count, CAP, width).transpose(1, 0, 2, 3).reshape(block_count, EXPERTS * CAP, width)


def section_pass(inputs, cotangents, route_table, weight_table, gate_w, up_w, down_w, with_gradient):
    block_count = TOKENS // TOK_DEV
    width = inputs.shape[-1]
    input_blocks = inputs.reshape(block_count, TOK_DEV, width)
    route_blocks = route_table.reshape(block_count, TOK_DEV, TOP)
    weight_blocks = weight_table.reshape(block_count, TOK_DEV, TOP)
    targets, source_row, filled = jax.vmap(lambda block: slot_plan(block, EXPERTS, CAP))(route_blocks)
    packed_inputs = to_experts(jax.vmap(pack_rows)(input_blocks, source_row, filled), block_count)
    if with_gradient:
        cot_blocks = cotangents.reshape(block_count, TOK_DEV, width)
        packed_cots = to_experts(jax.vmap(pack_rows)(cot_blocks, source_row, filled), block_count)
        expert_results = lax.map(lambda operands: expert_backward(*operands), (packed_inputs, packed_cots, gate_w, up_w, down_w))
        base = cotangents
    else:
        expert_results = lax.map(lambda operands: expert_forward(*operands), (packed_inputs, gate_w, up_w, down_w))
        base = inputs
    returned = from_experts(expert_results, block_count)
    mixed = jax.vmap(gate_combine)(returned, targets, weight_blocks)
    return base.astype(jnp.float32) + mixed.reshape(TOKENS, width)


def reference(forward_inputs, backward_inputs, backward_cotangents, routes, route_weights, w_gate, w_up, w_down):
    forward_out = [section_pass(forward_inputs[section], None, routes[0, section], route_weights[0, section], w_gate[section], w_up[section], w_down[section], False) for section in range(2)]
    backward_out = [section_pass(backward_inputs[section], backward_cotangents[section], routes[1, section], route_weights[1, section], w_gate[section], w_up[section], w_down[section], True) for section in range(2)]
    finished = jnp.stack([backward_out[0], forward_out[1]]).astype(jnp.bfloat16)
    handed = jnp.stack([backward_out[1], forward_out[0]]).astype(jnp.bfloat16)
    return finished, handed
```

```python
import functools

import jax
import jax.numpy as jnp
from jax import lax
from jax.experimental import pallas as pl
from jax.experimental.pallas import tpu as pltpu
from jax.sharding import PartitionSpec as P

MESH = pl.DeviceIdType.MESH
F32 = jnp.float32
BF16 = jnp.bfloat16

TOK = 128
CAP = 17
SRC = 8
DST = 8
BLK = 144
TILES = BLK // 16
FAR = (2, 1, 3)
DIRECT = (96, 32, 32)
REDUCE = (32, 96)


def dot(left, right):
    return jnp.dot(left, right, preferred_element_type=F32)


def dot_nt(left, right):
    return lax.dot_general(left, right, (((1,), (1,)), ((), ())), preferred_element_type=F32)


def dot_tn(left, right):
    return lax.dot_general(left, right, (((0,), (0,)), ((), ())), preferred_element_type=F32)


def kernel(
    xf, xb, xc, routes, weights, wg_hbm, wu_hbm, wd_hbm,
    out_f, out_b, gathered,
    town, table, gt, packed, recv, back, c_left, c_right, f_y, f_a, acc, hid, wg, wu, wd,
    w_sem, fetch_sem, loc_sem, oloc_sem,
    t_s, t_r, g1_s, g1_r, g2_s, g2_r, g3_s, g3_r, g4_s, g4_r, a_s, a_r, o_s, o_r,
    c1_s, c1_r, c2_s, c2_r, c3_s, c3_r, c4_s, c4_r,
):
    seg = lax.axis_index("segment")
    me = lax.axis_index("expert")
    z, y, x, c = me // 16, (me // 8) % 2, (me // 2) % 4, me % 2
    a = z * (1 - c) + x * c
    b = x * (1 - c) + z * c
    inputs = (xf, xb, xc)

    def device(aa, yy, bb, cc):
        zz = aa * (1 - c) + bb * c
        xx = bb * (1 - c) + aa * c
        return (seg, ((zz * 2 + yy) * 4 + xx) * 2 + cc)

    def at_a(d, dy=0):
        return device((a + d) % 4, (y + dy) % 2, b, c)

    def source(d, dy=0):
        return ((a + d + 4) % 4) * 2 + (y + dy) % 2

    own = a * 2 + y

    def remote(src, dst, send, rec, to):
        return pltpu.make_async_remote_copy(
            src_ref=src, dst_ref=dst, send_sem=send, recv_sem=rec, device_id=to, device_id_type=MESH
        )

    loads = [
        pltpu.make_async_copy(src, dst, w_sem.at[i])
        for i, (src, dst) in enumerate(((wg_hbm, wg), (wu_hbm, wu), (wd_hbm, wd)))
    ]

    barrier = pltpu.get_barrier_semaphore()
    partners = [at_a(d, dy) for d in range(4) for dy in range(2) if d or dy]
    partners += [device(a, y, (b + d) % 4, c) for d in (1, 2, 3)]
    partners += [device(a, y, (b + d) % 4, 1 - c) for d in range(4)]
    partners += [device((a + d) % 4, y, b, 1 - c) for d in (1, 2, 3)]
    for to in partners:
        pl.semaphore_signal(barrier, inc=1, device_id=to, device_id_type=MESH)
    pl.semaphore_wait(barrier, len(partners))

    def g1(q):
        return remote(inputs[q], gathered.at[q, own], g1_s.at[q], g1_r.at[q], at_a(0, 1))

    def g2(q, d):
        return remote(inputs[q], gathered.at[q, own], g2_s.at[q, d], g2_r.at[q, d], at_a(d))

    def g3(q, d):
        part = gathered.at[q, source(0, 1), pl.ds(0, DIRECT[q])]
        return remote(part, part, g3_s.at[q, d], g3_r.at[q, d], at_a(d))

    def g4(q, d):
        part = gathered.at[q, source(-d), pl.ds(DIRECT[q], TOK - DIRECT[q])]
        return remote(part, part, g4_s.at[q, d], g4_r.at[q, d], at_a(0, 1))

    def gather_own(q):
        g1(q).start()
        for d in FAR:
            g2(q, d).start()

    def gather_relay(q):
        g1(q).wait_recv()
        for d in FAR:
            g3(q, d).start()
        for d in (1, 3, 2):
            g2(q, d).wait_recv()
            g4(q, d).start()

    def gather_rest(q):
        for d in FAR:
            g3(q, d).wait_recv()
            g4(q, d).wait_recv()

    gather_own(0)
    for load in loads:
        load.start()

    row = lax.broadcasted_iota(jnp.int32, (64, TOK), 0)
    ra, ry, rb, rc = row // 16, (row // 8) % 2, (row // 2) % 4, row % 2
    expert = (
        ((ra * (1 - c) + rb * c) * 2 + ry) * 4 + (rb * (1 - c) + ra * c)
    ) * 2 + rc
    before = (
        lax.broadcasted_iota(jnp.int32, (TOK, TOK), 0)
        < lax.broadcasted_iota(jnp.int32, (TOK, TOK), 1)
    ).astype(F32).astype(BF16)
    for p in range(2):
        named = jnp.zeros((64, TOK), F32)
        weight = jnp.zeros((64, TOK), F32)
        for j in range(8):
            hit = routes[p, j : j + 1, :] == expert
            named = jnp.where(hit, 1.0, named)
            weight = jnp.where(hit, weights[p, j : j + 1, :], weight)
        prior = dot(named.astype(BF16), before)
        place = jnp.where(named > 0.5, prior, -1000.0)
        for g in range(8):
            town[g, 2 * p] = place[8 * g : 8 * g + 8]
            town[g, 2 * p + 1] = weight[8 * g : 8 * g + 8]

    def send_table(d, dy):
        return remote(
            town.at[source(d, dy)], table.at[own], t_s.at[2 * d + dy], t_r.at[2 * d + dy], at_a(d, dy)
        )

    near = [(d, dy) for d in range(4) for dy in range(2) if d or dy]
    for d, dy in near:
        send_table(d, dy).start()
    table[own] = town[own]

    def fetch(q, d, dy):
        s = source(d, dy)
        src = inputs[q] if (d, dy) == (0, 0) else gathered.at[q, s]
        return pltpu.make_async_copy(src, gt.at[s], fetch_sem.at[2 * d + dy])

    slot_row = lax.broadcasted_iota(jnp.int32, (DST, 16, TOK), 1).astype(F32)

    def pack(q, buf):
        def step(i, carry):
            s0 = jnp.clip(i - 1, 0, SRC - 2)
            parts = []
            for o in range(2):
                place = table[s0 + o, 2 * min(q, 1)]
                shift = (CAP * (s0 + o) - 16 * i).astype(F32)
                parts.append(
                    jnp.where(place[:, None, :] + shift == slot_row, 1.0, 0.0).reshape(DST * 16, TOK)
                )
            pick = jnp.concatenate(parts, axis=1).astype(BF16)
            rows = gt[pl.ds(s0, 2)].reshape(2 * TOK, 2048)
            made = dot(pick, rows).astype(BF16).reshape(DST, 16, 2048)
            packed[buf, :, pl.ds(pl.multiple_of(16 * i, 16), 16), :] = made
            return carry

        lax.fori_loop(0, TILES, step, 0)

    near_b = [(d, dc) for d in (2, 1, 3, 0) for dc in range(2) if d or dc]

    def scatter(q, buf, d, dc):
        bb, cc = (b + d) % 4, (c + dc) % 2
        return remote(
            packed.at[buf, bb * 2 + cc], recv.at[q, 2 * d + dc], a_s.at[q, 2 * d + dc],
            a_r.at[q, 2 * d + dc], device(a, y, bb, cc),
        )

    def scatter_own(q, buf):
        return pltpu.make_async_copy(packed.at[buf, b * 2 + c], recv.at[q, 0], loc_sem.at[q])

    def pack_and_send(q, buf):
        for d in range(4):
            for dy in range(2):
                fetch(q, d, dy).start()
        for d in range(4):
            for dy in range(2):
                fetch(q, d, dy).wait()
        pack(q, buf)
        for d, dc in near_b:
            scatter(q, buf, d, dc).start()
        scatter_own(q, buf).start()

    def scatter_wait(q, buf, k):
        @pl.when(k == 0)
        def _():
            scatter_own(q, buf).wait()

        @pl.when(k > 0)
        def _():
            scatter(q, buf, k, 0).wait_recv()

        scatter(q, buf, k, 1).wait_recv()

    def result_same(q, p, k):
        return remote(
            recv.at[q, 2 * k], back.at[p, b * 2 + c], o_s.at[p, 2 * k], o_r.at[p, 2 * k],
            device(a, y, (b - k + 4) % 4, c),
        )

    def result_other(q, p, k):
        return remote(
            recv.at[q, 2 * k + 1], back.at[p, a * 2 + c], o_s.at[p, 2 * k + 1], o_r.at[p, 2 * k + 1],
            device((a - k + 4) % 4, y, b, 1 - c),
        )

    def result_own(q, p):
        return pltpu.make_async_copy(recv.at[q, 0], back.at[p, b * 2 + c], oloc_sem.at[p])

    def send_results(q, p, k):
        @pl.when(k == 0)
        def _():
            result_own(q, p).start()

        @pl.when(k > 0)
        def _():
            result_same(q, p, k).start()

        result_other(q, p, k).start()

    def results_wait(q, p):
        result_own(q, p).wait()
        for k in range(4):
            if k:
                result_same(q, p, k).wait_recv()
            result_other(q, p, k).wait_recv()

    def forward_step(k, carry):
        scatter_wait(0, 0, k)
        rows = recv[0, pl.ds(2 * k, 2)].reshape(2 * BLK, 2048)
        for n in range(3):
            cols = slice(256 * n, 256 * n + 256)
            gate = dot(rows, wg[:, cols])
            up = dot(rows, wu[:, cols])
            hid[0, :, cols] = (gate * jax.nn.sigmoid(gate) * up).astype(BF16)
        for n in range(4):
            cols = slice(512 * n, 512 * n + 512)
            recv[0, pl.ds(2 * k, 2), :, cols] = (
                dot(hid[0], wd[:, cols]).astype(BF16).reshape(2, BLK, 512)
            )
        send_results(0, 0, k)
        return carry

    def backward_step(k, carry):
        scatter_wait(1, 1, k)
        scatter_wait(2, 0, k)
        rows = recv[1, pl.ds(2 * k, 2)].reshape(2 * BLK, 2048)
        cot = recv[2, pl.ds(2 * k, 2)].reshape(2 * BLK, 2048)
        for n in range(3):
            cols = slice(256 * n, 256 * n + 256)
            gate = dot(rows, wg[:, cols])
            up = dot(rows, wu[:, cols])
            grad = dot_nt(cot, wd[cols, :])
            sig = jax.nn.sigmoid(gate)
            hid[0, :, cols] = (grad * up * sig * (1.0 + gate * (1.0 - sig))).astype(BF16)
            hid[1, :, cols] = (grad * gate * sig).astype(BF16)
        for n in range(4):
            cols = slice(512 * n, 512 * n + 512)
            recv[1, pl.ds(2 * k, 2), :, cols] = (
                (dot_nt(hid[0], wg[cols, :]) + dot_nt(hid[1], wu[cols, :]))
                .astype(BF16)
                .reshape(2, BLK, 512)
            )
        send_results(1, 1, k)
        return carry

    pair_row = lax.broadcasted_iota(jnp.int32, (DST, 32, TOK), 1).astype(F32)

    def partial(p, d, dy):
        s = source(d, dy)
        place = table[s, 2 * p]
        weight = table[s, 2 * p + 1]
        hit = place[:, None, :] + s.astype(F32) == pair_row
        mix = jnp.where(hit, weight[:, None, :], 0.0).reshape(DST * 32, TOK).astype(BF16)
        rows = back[p, :, pl.ds(pl.multiple_of(16 * s, 16), 32), :].reshape(DST * 32, 2048)
        return dot_tn(mix, rows)

    sums = gt

    def c1(p, d):
        cut = REDUCE[p]
        return remote(
            sums.at[2 * d + 1, pl.ds(0, cut)], c_left.at[p, d - 1, pl.ds(0, cut)],
            c1_s.at[p, d], c1_r.at[p, d], at_a(d),
        )

    def c2(p, d):
        cut = REDUCE[p]
        rest = pl.ds(cut, TOK - cut)
        dst = c_right.at[p, d - 1, rest] if d else f_y.at[p, rest]
        return remote(sums.at[2 * d + 1, rest], dst, c2_s.at[p, d], c2_r.at[p, d], at_a(0, 1))

    def c3(p):
        part = pl.ds(0, REDUCE[p])
        return remote(sums.at[1, part], f_y.at[p, part], c3_s.at[p], c3_r.at[p], at_a(0, 1))

    def c4(p, d):
        return remote(sums.at[2 * d], f_a.at[p, d - 1], c4_s.at[p, d], c4_r.at[p, d], at_a(d))

    def combine_start(p):
        for d in (2, 1, 3):
            sums[2 * d + 1] = partial(p, d, 1).astype(BF16)
            c1(p, d).start()
            c2(p, d).start()
        sums[1] = partial(p, 0, 1).astype(BF16)
        c2(p, 0).start()
        for d in (2, 1, 3):
            sums[2 * d] = partial(p, d, 0).astype(BF16)
        acc[...] = partial(p, 0, 0) + inputs[2 * p][...].astype(F32)

    def combine_middle(p):
        cut = REDUCE[p]
        for d in (2, 1, 3):
            c2(p, d).wait_recv()
            sums[2 * d, cut:, :] = (
                sums[2 * d, cut:, :].astype(F32) + c_right[p, d - 1, cut:, :].astype(F32)
            ).astype(BF16)
            c4(p, d).start()
        for d in (1, 3, 2):
            c1(p, d).wait_recv()
        total = sums[1, :cut, :].astype(F32)
        for d in (1, 2, 3):
            total += c_left[p, d - 1, :cut, :].astype(F32)
        sums[1, :cut, :] = total.astype(BF16)
        c3(p).start()

    def combine_end(p, out):
        for d in (1, 3, 2):
            c4(p, d).wait_recv()
        c2(p, 0).wait_recv()
        c3(p).wait_recv()
        total = acc[...] + f_y[p].astype(F32)
        for d in (1, 2, 3):
            total += f_a[p, d - 1].astype(F32)
        out[...] = total.astype(BF16)

    def combine_sent(p):
        for d in range(4):
            if d:
                c1(p, d).wait_send()
                c4(p, d).wait_send()
            c2(p, d).wait_send()
        c3(p).wait_send()

    gather_relay(0)
    gather_own(1)
    gather_rest(0)
    for d, dy in near:
        send_table(d, dy).wait_recv()
    pack_and_send(0, 0)
    gather_relay(1)
    gather_own(2)
    gather_rest(1)
    pack_and_send(1, 1)
    gather_relay(2)
    for load in loads:
        load.wait()
    lax.fori_loop(0, 4, forward_step, 0)
    gather_rest(2)
    for d, dc in near_b:
        scatter(0, 0, d, dc).wait_send()
    pack_and_send(2, 0)
    results_wait(0, 0)
    combine_start(0)
    lax.fori_loop(0, 4, backward_step, 0)
    combine_middle(0)
    combine_end(0, out_f)
    combine_sent(0)
    results_wait(1, 1)
    combine_start(1)
    combine_middle(1)
    combine_end(1, out_b)
    combine_sent(1)

    for d, dy in near:
        send_table(d, dy).wait_send()
    for q in range(3):
        g1(q).wait_send()
        for d in FAR:
            g2(q, d).wait_send()
            g3(q, d).wait_send()
            g4(q, d).wait_send()
    for d, dc in near_b:
        scatter(1, 1, d, dc).wait_send()
        scatter(2, 0, d, dc).wait_send()
    for q in range(2):
        for k in range(4):
            if k:
                result_same(q, q, k).wait_send()
            result_other(q, q, k).wait_send()


def moe(xf, xb, xc, routes, weights, wg, wu, wd):
    vmem = pl.BlockSpec(memory_space=pltpu.VMEM)
    hbm = pl.BlockSpec(memory_space=pl.ANY)
    dma = pltpu.SemaphoreType.DMA
    block = (TOK, 2048)
    out_f, out_b, _ = pl.pallas_call(
        kernel,
        out_shape=(
            jax.ShapeDtypeStruct(block, BF16),
            jax.ShapeDtypeStruct(block, BF16),
            jax.ShapeDtypeStruct((3, SRC) + block, BF16),
        ),
        in_specs=[vmem] * 5 + [hbm] * 3,
        out_specs=(vmem, vmem, hbm),
        scratch_shapes=[
            pltpu.VMEM((8, 4, 8, TOK), F32),
            pltpu.VMEM((8, 4, 8, TOK), F32),
            pltpu.VMEM((SRC,) + block, BF16),
            pltpu.VMEM((2, DST, BLK, 2048), BF16),
            pltpu.VMEM((3, 8, BLK, 2048), BF16),
            pltpu.VMEM((2, DST, BLK, 2048), BF16),
            pltpu.VMEM((2, 3) + block, BF16),
            pltpu.VMEM((2, 3) + block, BF16),
            pltpu.VMEM((2,) + block, BF16),
            pltpu.VMEM((2, 3) + block, BF16),
            pltpu.VMEM(block, F32),
            pltpu.VMEM((2, 2 * BLK, 768), BF16),
            pltpu.VMEM((2048, 768), BF16),
            pltpu.VMEM((2048, 768), BF16),
            pltpu.VMEM((768, 2048), BF16),
            dma((3,)), dma((8,)), dma((3,)), dma((2,)),
            dma((8,)), dma((8,)),
            dma((3,)), dma((3,)),
            dma((3, 4)), dma((3, 4)),
            dma((3, 4)), dma((3, 4)),
            dma((3, 4)), dma((3, 4)),
            dma((3, 8)), dma((3, 8)),
            dma((2, 8)), dma((2, 8)),
            dma((2, 4)), dma((2, 4)),
            dma((2, 4)), dma((2, 4)),
            dma((2,)), dma((2,)),
            dma((2, 4)), dma((2, 4)),
        ],
        compiler_params=pltpu.CompilerParams(
            collective_id=0, has_side_effects=True, vmem_limit_bytes=63 * 2**20
        ),
    )(xf, xb, xc, routes, weights, wg, wu, wd)
    return out_f, out_b


def per_device(
    forward_inputs,
    backward_inputs,
    backward_cotangents,
    routes,
    route_weights,
    w_gate,
    w_up,
    w_down,
):
    forward_out, backward_out = moe(
        forward_inputs[0],
        backward_inputs[0],
        backward_cotangents[0],
        routes[:, 0].transpose(0, 2, 1),
        route_weights[:, 0].transpose(0, 2, 1),
        w_gate[0, 0],
        w_up[0, 0],
        w_down[0, 0],
    )
    first_segment = lax.axis_index("segment") == 0
    finished = jnp.where(first_segment, backward_out, forward_out)
    handed = lax.ppermute(
        jnp.where(first_segment, forward_out, backward_out), "segment", [(0, 1), (1, 0)]
    )
    return (finished[None], handed[None])


def solution(mesh):
    placed = (
        P("segment", "expert", None),
        P("segment", "expert", None),
        P("segment", "expert", None),
        P(None, "segment", "expert", None),
        P(None, "segment", "expert", None),
        P("segment", "expert", None, None),
        P("segment", "expert", None, None),
        P("segment", "expert", None, None),
    )
    return jax.shard_map(
        per_device,
        mesh=mesh,
        in_specs=placed,
        out_specs=(P("segment", "expert", None), P("segment", "expert", None)),
        check_vma=False,
    )
```

```python
import functools

import jax
import jax.numpy as jnp
from jax import lax
from jax.experimental import pallas as pl
from jax.experimental.pallas import tpu as pltpu
from jax.sharding import PartitionSpec as P

MESH = pl.DeviceIdType.MESH
F32 = jnp.float32
BF16 = jnp.bfloat16

TOK = 128
CAP = 17
SRC = 8
DST = 8
BLK = 144
TILES = BLK // 16
FAR = (2, 1, 3)
DIRECT = (32, 64, 32)
REDUCE = (96, 32)
PARTS = 2
WIDE = 2048 // PARTS
SLOTS = 4


def dot(left, right):
    return jnp.dot(left, right, preferred_element_type=F32)


def dot_nt(left, right):
    return lax.dot_general(left, right, (((1,), (1,)), ((), ())), preferred_element_type=F32)


def dot_tn(left, right):
    return lax.dot_general(left, right, (((0,), (0,)), ((), ())), preferred_element_type=F32)


def kernel(
    xf, xb, xc, routes, weights, wg_hbm, wu_hbm, wd_hbm,
    finished, handed, gathered,
    town, table, gt, packed, recv, back, crossed, f_y, f_a, acc, ready, hid, wg, wu, wd,
    w_sem, fetch_sem, loc_sem, keep_sem, oloc_sem,
    t_s, t_r, g1_s, g1_r, g2_s, g2_r, g2f_s, g2f_r, g3_s, g3_r, g3f_s, g3f_r, g4_s, g4_r, a_s, a_r, o_s, o_r,
    c1_s, c1_r, c2_s, c2_r, c3_s, c3_r, c4_s, c4_r, h_s, h_r,
):
    seg = lax.axis_index("segment")
    me = lax.axis_index("expert")
    z, y, x, c = me // 16, (me // 8) % 2, (me // 2) % 4, me % 2
    a = z * (1 - c) + x * c
    b = x * (1 - c) + z * c
    inputs = (xf, xb, xc)

    def device(aa, yy, bb, cc):
        zz = aa * (1 - c) + bb * c
        xx = bb * (1 - c) + aa * c
        return (seg, ((zz * 2 + yy) * 4 + xx) * 2 + cc)

    def at_a(d, dy=0):
        return device((a + d) % 4, (y + dy) % 2, b, c)

    def source(d, dy=0):
        return ((a + d + 4) % 4) * 2 + (y + dy) % 2

    own = a * 2 + y

    def remote(src, dst, send, rec, to):
        return pltpu.make_async_remote_copy(
            src_ref=src, dst_ref=dst, send_sem=send, recv_sem=rec, device_id=to, device_id_type=MESH
        )

    loads = [
        pltpu.make_async_copy(src, dst, w_sem.at[i])
        for i, (src, dst) in enumerate(((wg_hbm, wg), (wu_hbm, wu), (wd_hbm, wd)))
    ]

    barrier = pltpu.get_barrier_semaphore()
    partners = [at_a(d, dy) for d in range(4) for dy in range(2) if d or dy]
    partners += [device(a, y, (b + d) % 4, c) for d in (1, 2, 3)]
    partners += [device(a, y, (b + d) % 4, 1 - c) for d in range(4)]
    partners += [device((a + d) % 4, y, b, 1 - c) for d in (1, 2, 3)]
    partners += [(1 - seg, me)]
    for to in partners:
        pl.semaphore_signal(barrier, inc=1, device_id=to, device_id_type=MESH)
    pl.semaphore_wait(barrier, len(partners))

    def columns(h):
        return pl.ds(WIDE * h, WIDE)

    def g1(q, h):
        return remote(
            inputs[q].at[:, columns(h)], gathered.at[q, h, own], g1_s.at[q, h], g1_r.at[q, h], at_a(0, 1)
        )

    def g2(q, h, d):
        return remote(
            inputs[q].at[:, columns(h)], gathered.at[q, h, own], g2_s.at[q, h, d], g2_r.at[q, h, d],
            at_a(d),
        )

    def g2f(q, h, d):
        part = gathered.at[q, h, source(-d), pl.ds(0 if d == 1 else TOK // 2, TOK // 2)]
        return remote(part, part, g2f_s.at[q, h, d], g2f_r.at[q, h, d], at_a(d))

    def g3(q, h, d):
        part = gathered.at[q, h, source(0, 1), pl.ds(0, DIRECT[q])]
        return remote(part, part, g3_s.at[q, h, d], g3_r.at[q, h, d], at_a(d))

    def g3f(q, h, d):
        half = DIRECT[q] // 2
        part = gathered.at[q, h, source(-d, 1), pl.ds(0 if d == 1 else half, half)]
        return remote(part, part, g3f_s.at[q, h, d], g3f_r.at[q, h, d], at_a(d))

    def g4(q, h, d):
        part = gathered.at[q, h, source(-d), pl.ds(DIRECT[q], TOK - DIRECT[q])]
        return remote(part, part, g4_s.at[q, h, d], g4_r.at[q, h, d], at_a(0, 1))

    def fetch(q, h, d, dy):
        s = source(d, dy)
        src = inputs[q].at[:, columns(h)] if (d, dy) == (0, 0) else gathered.at[q, h, s]
        return pltpu.make_async_copy(src, gt.at[h, s], fetch_sem.at[h, 2 * d + dy])

    def gather_own(q, h):
        g1(q, h).start()
        for d in (1, 3):
            g2(q, h, d).start()

    def gather_relay(q, h):
        g1(q, h).wait_recv()
        for d in (1, 3):
            g3(q, h, d).start()
        for d in (1, 3):
            g2(q, h, d).wait_recv()
            g2f(q, h, d).start()
            g4(q, h, d).start()

    def gather_onward(q, h):
        for d in (1, 3):
            g3(q, h, d).wait_recv()
            g3f(q, h, d).start()
        for d in (1, 3):
            g2f(q, h, d).wait_recv()
        g4(q, h, 2).start()
        for dy in range(2):
            fetch(q, h, 0, dy).start()
        for d in range(1, 4):
            fetch(q, h, d, 0).start()

    def gather_rest(q, h):
        for d in (1, 3):
            g4(q, h, d).wait_recv()
            fetch(q, h, 4 - d, 1).start()
        for d in (1, 3):
            g3f(q, h, d).wait_recv()
        g4(q, h, 2).wait_recv()
        fetch(q, h, 2, 1).start()

    def gather_sent(q, h):
        g1(q, h).wait_send()
        for d in (1, 3):
            g2(q, h, d).wait_send()
            g2f(q, h, d).wait_send()
            g3(q, h, d).wait_send()
            g3f(q, h, d).wait_send()
        for d in FAR:
            g4(q, h, d).wait_send()

    units = [(q, h) for q in (1, 2, 0) for h in range(PARTS)]
    gather_own(*units[0])
    for load in loads:
        load.start()

    row = lax.broadcasted_iota(jnp.int32, (64, TOK), 0)
    ra, ry, rb, rc = row // 16, (row // 8) % 2, (row // 2) % 4, row % 2
    expert = (
        ((ra * (1 - c) + rb * c) * 2 + ry) * 4 + (rb * (1 - c) + ra * c)
    ) * 2 + rc
    before = (
        lax.broadcasted_iota(jnp.int32, (TOK, TOK), 0)
        < lax.broadcasted_iota(jnp.int32, (TOK, TOK), 1)
    ).astype(F32).astype(BF16)
    for p in range(2):
        named = jnp.zeros((64, TOK), F32)
        weight = jnp.zeros((64, TOK), F32)
        for j in range(8):
            hit = routes[p, j : j + 1, :] == expert
            named = jnp.where(hit, 1.0, named)
            weight = jnp.where(hit, weights[p, j : j + 1, :], weight)
        prior = dot(named.astype(BF16), before)
        place = jnp.where(named > 0.5, prior, -1000.0)
        for g in range(8):
            town[g, 2 * p] = place[8 * g : 8 * g + 8]
            town[g, 2 * p + 1] = weight[8 * g : 8 * g + 8]

    def send_table(d, dy):
        return remote(
            town.at[source(d, dy)], table.at[own], t_s.at[2 * d + dy], t_r.at[2 * d + dy], at_a(d, dy)
        )

    near = [(d, dy) for d in range(4) for dy in range(2) if d or dy]
    for d, dy in near:
        send_table(d, dy).start()
    table[own] = town[own]

    slot_row = lax.broadcasted_iota(jnp.int32, (DST, 16, TOK), 1).astype(F32)

    def pack(q, h, buf):
        def step(i, carry):
            s0 = jnp.clip(i - 1, 0, SRC - 2)
            parts = []
            for o in range(2):
                place = table[s0 + o, 2 * min(q, 1)]
                shift = (CAP * (s0 + o) - 16 * i).astype(F32)
                parts.append(
                    jnp.where(place[:, None, :] + shift == slot_row, 1.0, 0.0).reshape(DST * 16, TOK)
                )
            pick = jnp.concatenate(parts, axis=1).astype(BF16)
            rows = gt[h, pl.ds(s0, 2)].reshape(2 * TOK, WIDE)
            made = dot(pick, rows).astype(BF16).reshape(DST, 16, WIDE)
            packed[buf, :, pl.ds(pl.multiple_of(16 * i, 16), 16), :] = made
            return carry

        lax.fori_loop(0, TILES, step, 0)

    near_b = [(d, dc) for d in (2, 1, 3, 0) for dc in range(2) if d or dc]

    def scatter(q, h, d, dc):
        buf = units.index((q, h)) % SLOTS
        bb, cc = (b + d) % 4, (c + dc) % 2
        return remote(
            packed.at[buf, bb * 2 + cc], recv.at[q, 2 * d + dc, :, columns(h)],
            a_s.at[q, h, 2 * d + dc], a_r.at[q, h, 2 * d + dc], device(a, y, bb, cc),
        )

    def scatter_own(q, h):
        buf = units.index((q, h)) % SLOTS
        return pltpu.make_async_copy(
            packed.at[buf, b * 2 + c], recv.at[q, 0, :, columns(h)], loc_sem.at[q, h]
        )

    def scatter_sent(q, h):
        for d, dc in near_b:
            scatter(q, h, d, dc).wait_send()
        scatter_own(q, h).wait()

    def pack_and_send(q, h):
        for d in range(4):
            for dy in range(2):
                fetch(q, h, d, dy).wait()
        pack(q, h, units.index((q, h)) % SLOTS)
        for d, dc in near_b:
            scatter(q, h, d, dc).start()
        scatter_own(q, h).start()

    def scatter_wait(q, k):
        for h in range(PARTS):

            @pl.when(k > 0)
            def _():
                scatter(q, h, k, 0).wait_recv()

            scatter(q, h, k, 1).wait_recv()

    def result_same(p, h, k):
        return remote(
            recv.at[p, 2 * k, :, columns(h)], back.at[p, b * 2 + c, :, columns(h)],
            o_s.at[p, h, 2 * k], o_r.at[p, h, 2 * k], device(a, y, (b - k + 4) % 4, c),
        )

    def result_other(p, h, k):
        return remote(
            recv.at[p, 2 * k + 1, :, columns(h)], back.at[p, a * 2 + c, :, columns(h)],
            o_s.at[p, h, 2 * k + 1], o_r.at[p, h, 2 * k + 1], device((a - k + 4) % 4, y, b, 1 - c),
        )

    def result_own(p, h):
        return pltpu.make_async_copy(
            recv.at[p, 0, :, columns(h)], back.at[p, b * 2 + c, :, columns(h)], oloc_sem.at[p, h]
        )

    def send_results(p, h, k):
        @pl.when(k == 0)
        def _():
            result_own(p, h).start()

        @pl.when(k > 0)
        def _():
            result_same(p, h, k).start()

        result_other(p, h, k).start()

    def results_wait(p, h):
        result_own(p, h).wait()
        for k in range(4):
            if k:
                result_same(p, h, k).wait_recv()
            result_other(p, h, k).wait_recv()

    def results_sent(p, h):
        for k in range(4):
            if k:
                result_same(p, h, k).wait_send()
            result_other(p, h, k).wait_send()

    def forward_hidden(k):
        scatter_wait(0, k)
        rows = recv[0, pl.ds(2 * k, 2)].reshape(2 * BLK, 2048)
        for n in range(3):
            cols = slice(256 * n, 256 * n + 256)
            gate = dot(rows, wg[:, cols])
            up = dot(rows, wu[:, cols])
            hid[0, k, :, cols] = (gate * jax.nn.sigmoid(gate) * up).astype(BF16)

    def forward_part(h, k):
        for n in range(WIDE // 512):
            cols = slice(WIDE * h + 512 * n, WIDE * h + 512 * n + 512)
            recv[0, pl.ds(2 * k, 2), :, cols] = (
                dot(hid[0, k], wd[:, cols]).astype(BF16).reshape(2, BLK, 512)
            )
        send_results(0, h, k)

    def backward_hidden(k):
        scatter_wait(1, k)
        scatter_wait(2, k)
        rows = recv[1, pl.ds(2 * k, 2)].reshape(2 * BLK, 2048)
        cot = recv[2, pl.ds(2 * k, 2)].reshape(2 * BLK, 2048)
        for n in range(3):
            cols = slice(256 * n, 256 * n + 256)
            gate = dot(rows, wg[:, cols])
            up = dot(rows, wu[:, cols])
            grad = dot_nt(cot, wd[cols, :])
            sig = jax.nn.sigmoid(gate)
            hid[0, k, :, cols] = (grad * up * sig * (1.0 + gate * (1.0 - sig))).astype(BF16)
            hid[1, k, :, cols] = (grad * gate * sig).astype(BF16)

    def backward_part(h, k):
        for n in range(WIDE // 512):
            cols = slice(WIDE * h + 512 * n, WIDE * h + 512 * n + 512)
            recv[1, pl.ds(2 * k, 2), :, cols] = (
                (dot_nt(hid[0, k], wg[cols, :]) + dot_nt(hid[1, k], wu[cols, :]))
                .astype(BF16)
                .reshape(2, BLK, 512)
            )
        send_results(1, h, k)

    def loop(*steps):
        def body(k, carry):
            for step in steps:
                step(k)
            return carry

        lax.fori_loop(0, 4, body, 0)

    pair_row = lax.broadcasted_iota(jnp.int32, (DST, 32, TOK), 1).astype(F32)

    def partial(p, h, d, dy):
        s = source(d, dy)
        place = table[s, 2 * p]
        weight = table[s, 2 * p + 1]
        hit = place[:, None, :] + s.astype(F32) == pair_row
        mix = jnp.where(hit, weight[:, None, :], 0.0).reshape(DST * 32, TOK).astype(BF16)
        rows = back[p, :, pl.ds(pl.multiple_of(16 * s, 16), 32), columns(h)]
        return dot_tn(mix, rows.reshape(DST * 32, WIDE))

    sums = gt

    def c1(p, h, d):
        part = pl.ds(0, REDUCE[p])
        return remote(
            sums.at[h, 2 * d + 1, part], crossed.at[p, d - 1, part, columns(h)],
            c1_s.at[p, h, d], c1_r.at[p, h, d], at_a(d),
        )

    def c2(p, h, d):
        part = pl.ds(REDUCE[p], TOK - REDUCE[p])
        dst = crossed.at[p, d - 1, part, columns(h)] if d else f_y.at[p, part, columns(h)]
        return remote(
            sums.at[h, 2 * d + 1, part], dst, c2_s.at[p, h, d], c2_r.at[p, h, d], at_a(0, 1)
        )

    def c3(p, h):
        part = pl.ds(0, REDUCE[p])
        return remote(
            sums.at[h, 1, part], f_y.at[p, part, columns(h)], c3_s.at[p, h], c3_r.at[p, h],
            at_a(0, 1),
        )

    def c4(p, h, d):
        return remote(
            sums.at[h, 2 * d], f_a.at[p, d - 1, :, columns(h)],
            c4_s.at[p, h, d], c4_r.at[p, h, d], at_a(d),
        )

    def combine_start(p, h):
        cols = columns(h)
        results_wait(p, h)
        for d in (2, 1, 3):
            sums[h, 2 * d + 1] = partial(p, h, d, 1).astype(BF16)
            c1(p, h, d).start()
            c2(p, h, d).start()
        sums[h, 1] = partial(p, h, 0, 1).astype(BF16)
        c2(p, h, 0).start()
        for d in (2, 1, 3):
            sums[h, 2 * d] = partial(p, h, d, 0).astype(BF16)
        acc[:, cols] = partial(p, h, 0, 0) + inputs[2 * p][:, cols].astype(F32)

    def combine_middle(p, h):
        cols = columns(h)
        cut = REDUCE[p]
        for d in (2, 1, 3):
            c2(p, h, d).wait_recv()
            sums[h, 2 * d, cut:, :] = (
                sums[h, 2 * d, cut:, :].astype(F32) + crossed[p, d - 1, cut:, cols].astype(F32)
            ).astype(BF16)
            c4(p, h, d).start()
        for d in (1, 3, 2):
            c1(p, h, d).wait_recv()
        total = sums[h, 1, :cut, :].astype(F32)
        for d in (1, 2, 3):
            total += crossed[p, d - 1, :cut, cols].astype(F32)
        sums[h, 1, :cut, :] = total.astype(BF16)
        c3(p, h).start()

    def hand(p, h):
        part = ready.at[p, :, columns(h)]
        return remote(part, handed.at[:, columns(h)], h_s.at[p, h], h_r.at[p, h], (1 - seg, me))

    def keep(p, h):
        return pltpu.make_async_copy(
            ready.at[p, :, columns(h)], finished.at[:, columns(h)], keep_sem.at[h]
        )

    def combine_end(p, h):
        cols = columns(h)
        for d in (1, 3, 2):
            c4(p, h, d).wait_recv()
        c2(p, h, 0).wait_recv()
        c3(p, h).wait_recv()
        total = acc[:, cols] + f_y[p, :, cols].astype(F32)
        for d in (1, 2, 3):
            total += f_a[p, d - 1, :, cols].astype(F32)
        ready[p, :, cols] = total.astype(BF16)

        @pl.when(seg == p)
        def _():
            hand(p, h).start()

        @pl.when(seg == 1 - p)
        def _():
            keep(p, h).start()

    def combine_sent(p, h):
        for d in range(4):
            if d:
                c1(p, h, d).wait_send()
                c4(p, h, d).wait_send()
            c2(p, h, d).wait_send()
        c3(p, h).wait_send()

    def stage(step, i):
        if i < len(units):
            step(*units[i])

    stage(gather_relay, 0)
    stage(gather_own, 1)
    stage(gather_onward, 0)
    stage(gather_relay, 1)
    stage(gather_own, 2)
    for i, unit in enumerate(units):
        gather_rest(*unit)
        if i == 0:
            for d, dy in near:
                send_table(d, dy).wait_recv()
        if i >= SLOTS:
            scatter_sent(*units[i - SLOTS])
        pack_and_send(*unit)
        stage(gather_onward, i + 1)
        stage(gather_relay, i + 2)
        stage(gather_own, i + 3)
    for load in loads:
        load.wait()
    for unit in units[-SLOTS:]:
        scatter_own(*unit).wait()
    loop(backward_hidden, functools.partial(backward_part, 0))
    for h in range(1, PARTS):
        loop(functools.partial(backward_part, h))
    for h in range(PARTS):
        combine_start(1, h)
    loop(forward_hidden, functools.partial(forward_part, 0))
    for h in range(PARTS):
        combine_middle(1, h)
    for h in range(1, PARTS):
        loop(functools.partial(forward_part, h))
    for h in range(PARTS):
        combine_end(1, h)
    for h in range(PARTS):
        combine_sent(1, h)
    for h in range(PARTS):
        combine_start(0, h)
        if h:
            combine_middle(0, h - 1)
    combine_middle(0, PARTS - 1)
    for h in range(PARTS):
        combine_end(0, h)
    for h in range(PARTS):
        combine_sent(0, h)

    for p in range(2):
        for h in range(PARTS):
            results_sent(p, h)

            @pl.when(seg == p)
            def _():
                hand(p, h).wait_send()

            @pl.when(seg == 1 - p)
            def _():
                keep(p, h).wait()
                hand(p, h).wait_recv()

    for d, dy in near:
        send_table(d, dy).wait_send()
    for q, h in units:
        gather_sent(q, h)
    for q, h in units[-SLOTS:]:
        for d, dc in near_b:
            scatter(q, h, d, dc).wait_send()


def moe(xf, xb, xc, routes, weights, wg, wu, wd):
    vmem = pl.BlockSpec(memory_space=pltpu.VMEM)
    hbm = pl.BlockSpec(memory_space=pl.ANY)
    dma = pltpu.SemaphoreType.DMA
    block = (TOK, 2048)
    finished, handed, _ = pl.pallas_call(
        kernel,
        out_shape=(
            jax.ShapeDtypeStruct(block, BF16),
            jax.ShapeDtypeStruct(block, BF16),
            jax.ShapeDtypeStruct((3, PARTS, SRC, TOK, WIDE), BF16),
        ),
        in_specs=[vmem] * 5 + [hbm] * 3,
        out_specs=(hbm, hbm, hbm),
        scratch_shapes=[
            pltpu.VMEM((8, 4, 8, TOK), F32),
            pltpu.VMEM((8, 4, 8, TOK), F32),
            pltpu.VMEM((PARTS, SRC, TOK, WIDE), BF16),
            pltpu.VMEM((SLOTS, DST, BLK, WIDE), BF16),
            pltpu.VMEM((3, 8, BLK, 2048), BF16),
            pltpu.VMEM((2, DST, BLK, 2048), BF16),
            pltpu.VMEM((2, 3) + block, BF16),
            pltpu.VMEM((2,) + block, BF16),
            pltpu.VMEM((2, 3) + block, BF16),
            pltpu.VMEM(block, F32),
            pltpu.VMEM((2,) + block, BF16),
            pltpu.VMEM((2, 4, 2 * BLK, 768), BF16),
            pltpu.VMEM((2048, 768), BF16),
            pltpu.VMEM((2048, 768), BF16),
            pltpu.VMEM((768, 2048), BF16),
            dma((3,)), dma((PARTS, 8)), dma((3, PARTS)), dma((PARTS,)), dma((2, PARTS)),
            dma((8,)), dma((8,)),
            dma((3, PARTS)), dma((3, PARTS)),
            dma((3, PARTS, 4)), dma((3, PARTS, 4)),
            dma((3, PARTS, 4)), dma((3, PARTS, 4)),
            dma((3, PARTS, 4)), dma((3, PARTS, 4)),
            dma((3, PARTS, 4)), dma((3, PARTS, 4)),
            dma((3, PARTS, 4)), dma((3, PARTS, 4)),
            dma((3, PARTS, 8)), dma((3, PARTS, 8)),
            dma((2, PARTS, 8)), dma((2, PARTS, 8)),
            dma((2, PARTS, 4)), dma((2, PARTS, 4)),
            dma((2, PARTS, 4)), dma((2, PARTS, 4)),
            dma((2, PARTS)), dma((2, PARTS)),
            dma((2, PARTS, 4)), dma((2, PARTS, 4)),
            dma((2, PARTS)), dma((2, PARTS)),
        ],
        compiler_params=pltpu.CompilerParams(
            collective_id=0, has_side_effects=True, vmem_limit_bytes=63 * 2**20
        ),
    )(xf, xb, xc, routes, weights, wg, wu, wd)
    return finished, handed


def per_device(
    forward_inputs,
    backward_inputs,
    backward_cotangents,
    routes,
    route_weights,
    w_gate,
    w_up,
    w_down,
):
    finished, handed = moe(
        forward_inputs[0],
        backward_inputs[0],
        backward_cotangents[0],
        routes[:, 0].transpose(0, 2, 1),
        route_weights[:, 0].transpose(0, 2, 1),
        w_gate[0, 0],
        w_up[0, 0],
        w_down[0, 0],
    )
    return (finished[None], handed[None])


def solution(mesh):
    placed = (
        P("segment", "expert", None),
        P("segment", "expert", None),
        P("segment", "expert", None),
        P(None, "segment", "expert", None),
        P(None, "segment", "expert", None),
        P("segment", "expert", None, None),
        P("segment", "expert", None, None),
        P("segment", "expert", None, None),
    )
    return jax.shard_map(
        per_device,
        mesh=mesh,
        in_specs=placed,
        out_specs=(P("segment", "expert", None), P("segment", "expert", None)),
        check_vma=False,
    )
```

```python
import functools

import jax
import jax.numpy as jnp
from jax import lax
from jax.experimental import pallas as pl
from jax.experimental.pallas import tpu as pltpu
from jax.sharding import PartitionSpec as P

MESH = pl.DeviceIdType.MESH
F32 = jnp.float32
BF16 = jnp.bfloat16

TOK = 128
CAP = 17
SRC = 8
DST = 8
BLK = 144
TILES = BLK // 16
FAR = (2, 1, 3)
DIRECT = (32, 96, 32)
REDUCE = (96, 16)
PARTS = 2
WIDE = 2048 // PARTS
SLOTS = 4


def dot(left, right):
    return jnp.dot(left, right, preferred_element_type=F32)


def dot_nt(left, right):
    return lax.dot_general(left, right, (((1,), (1,)), ((), ())), preferred_element_type=F32)


def dot_tn(left, right):
    return lax.dot_general(left, right, (((0,), (0,)), ((), ())), preferred_element_type=F32)


def kernel(
    xf, xb, xc, routes, weights, wg_hbm, wu_hbm, wd_hbm,
    finished, handed, gathered,
    town, table, gt, packed, recv, back, crossed, f_y, f_a, acc, ready, hid, wg, wu, wd,
    w_sem, fetch_sem, loc_sem, oloc_sem,
    t_s, t_r, g1_s, g1_r, g2_s, g2_r, g2f_s, g2f_r, g3_s, g3_r, g3f_s, g3f_r, g4_s, g4_r, a_s, a_r, o_s, o_r,
    c1_s, c1_r, c2_s, c2_r, c3_s, c3_r, c4_s, c4_r, h_s, h_r,
):
    seg = lax.axis_index("segment")
    me = lax.axis_index("expert")
    z, y, x, c = me // 16, (me // 8) % 2, (me // 2) % 4, me % 2
    a = z * (1 - c) + x * c
    b = x * (1 - c) + z * c
    inputs = (xf, xb, xc)

    def device(aa, yy, bb, cc):
        zz = aa * (1 - c) + bb * c
        xx = bb * (1 - c) + aa * c
        return (seg, ((zz * 2 + yy) * 4 + xx) * 2 + cc)

    def at_a(d, dy=0):
        return device((a + d) % 4, (y + dy) % 2, b, c)

    def source(d, dy=0):
        return ((a + d + 4) % 4) * 2 + (y + dy) % 2

    own = a * 2 + y

    def remote(src, dst, send, rec, to):
        return pltpu.make_async_remote_copy(
            src_ref=src, dst_ref=dst, send_sem=send, recv_sem=rec, device_id=to, device_id_type=MESH
        )

    loads = [
        pltpu.make_async_copy(src, dst, w_sem.at[i])
        for i, (src, dst) in enumerate(((wg_hbm, wg), (wu_hbm, wu), (wd_hbm, wd)))
    ]

    barrier = pltpu.get_barrier_semaphore()
    partners = [at_a(d, dy) for d in range(4) for dy in range(2) if d or dy]
    partners += [device(a, y, (b + d) % 4, c) for d in (1, 2, 3)]
    partners += [device(a, y, (b + d) % 4, 1 - c) for d in range(4)]
    partners += [device((a + d) % 4, y, b, 1 - c) for d in (1, 2, 3)]
    partners += [(1 - seg, me)]
    for to in partners:
        pl.semaphore_signal(barrier, inc=1, device_id=to, device_id_type=MESH)
    pl.semaphore_wait(barrier, len(partners))

    def columns(h):
        return pl.ds(WIDE * h, WIDE)

    def g1(q, h):
        return remote(
            inputs[q].at[:, columns(h)], gathered.at[q, h, own], g1_s.at[q, h], g1_r.at[q, h], at_a(0, 1)
        )

    def g2(q, h, d):
        return remote(
            inputs[q].at[:, columns(h)], gathered.at[q, h, own], g2_s.at[q, h, d], g2_r.at[q, h, d],
            at_a(d),
        )

    def g2f(q, h, d):
        part = gathered.at[q, h, source(-d), pl.ds(0 if d == 1 else TOK // 2, TOK // 2)]
        return remote(part, part, g2f_s.at[q, h, d], g2f_r.at[q, h, d], at_a(d))

    def g3(q, h, d):
        part = gathered.at[q, h, source(0, 1), pl.ds(0, DIRECT[q])]
        return remote(part, part, g3_s.at[q, h, d], g3_r.at[q, h, d], at_a(d))

    def g3f(q, h, d):
        half = DIRECT[q] // 2
        part = gathered.at[q, h, source(-d, 1), pl.ds(0 if d == 1 else half, half)]
        return remote(part, part, g3f_s.at[q, h, d], g3f_r.at[q, h, d], at_a(d))

    def g4(q, h, d):
        part = gathered.at[q, h, source(-d), pl.ds(DIRECT[q], TOK - DIRECT[q])]
        return remote(part, part, g4_s.at[q, h, d], g4_r.at[q, h, d], at_a(0, 1))

    def fetch(q, h, d, dy):
        s = source(d, dy)
        src = inputs[q].at[:, columns(h)] if (d, dy) == (0, 0) else gathered.at[q, h, s]
        return pltpu.make_async_copy(src, gt.at[h, s], fetch_sem.at[h, 2 * d + dy])

    def gather_own(q, h):
        g1(q, h).start()
        for d in (1, 3):
            g2(q, h, d).start()

    def gather_relay(q, h):
        g1(q, h).wait_recv()
        for d in (1, 3):
            g3(q, h, d).start()
        for d in (1, 3):
            g2(q, h, d).wait_recv()
            g2f(q, h, d).start()
            g4(q, h, d).start()

    def gather_onward(q, h):
        for d in (1, 3):
            g3(q, h, d).wait_recv()
            g3f(q, h, d).start()
        for d in (1, 3):
            g2f(q, h, d).wait_recv()
        g4(q, h, 2).start()
        for dy in range(2):
            fetch(q, h, 0, dy).start()
        for d in range(1, 4):
            fetch(q, h, d, 0).start()

    def gather_rest(q, h):
        for d in (1, 3):
            g4(q, h, d).wait_recv()
            fetch(q, h, 4 - d, 1).start()
        for d in (1, 3):
            g3f(q, h, d).wait_recv()
        g4(q, h, 2).wait_recv()
        fetch(q, h, 2, 1).start()

    def gather_sent(q, h):
        g1(q, h).wait_send()
        for d in (1, 3):
            g2(q, h, d).wait_send()
            g2f(q, h, d).wait_send()
            g3(q, h, d).wait_send()
            g3f(q, h, d).wait_send()
        for d in FAR:
            g4(q, h, d).wait_send()

    units = [(q, h) for q in (1, 2, 0) for h in range(PARTS)]
    gather_own(*units[0])
    for load in loads:
        load.start()

    row = lax.broadcasted_iota(jnp.int32, (64, TOK), 0)
    ra, ry, rb, rc = row // 16, (row // 8) % 2, (row // 2) % 4, row % 2
    expert = (
        ((ra * (1 - c) + rb * c) * 2 + ry) * 4 + (rb * (1 - c) + ra * c)
    ) * 2 + rc
    before = (
        lax.broadcasted_iota(jnp.int32, (TOK, TOK), 0)
        < lax.broadcasted_iota(jnp.int32, (TOK, TOK), 1)
    ).astype(F32).astype(BF16)
    for p in range(2):
        named = jnp.zeros((64, TOK), F32)
        weight = jnp.zeros((64, TOK), F32)
        for j in range(8):
            hit = routes[p, j : j + 1, :] == expert
            named = jnp.where(hit, 1.0, named)
            weight = jnp.where(hit, weights[p, j : j + 1, :], weight)
        prior = dot(named.astype(BF16), before)
        place = jnp.where(named > 0.5, prior, -1000.0)
        for g in range(8):
            town[g, 2 * p] = place[8 * g : 8 * g + 8]
            town[g, 2 * p + 1] = weight[8 * g : 8 * g + 8]

    def send_table(d, dy):
        return remote(
            town.at[source(d, dy)], table.at[own], t_s.at[2 * d + dy], t_r.at[2 * d + dy], at_a(d, dy)
        )

    near = [(d, dy) for d in range(4) for dy in range(2) if d or dy]
    for d, dy in near:
        send_table(d, dy).start()
    table[own] = town[own]

    slot_row = lax.broadcasted_iota(jnp.int32, (DST, 16, TOK), 1).astype(F32)

    def pack(q, h, buf):
        def step(i, carry):
            s0 = jnp.clip(i - 1, 0, SRC - 2)
            parts = []
            for o in range(2):
                place = table[s0 + o, 2 * min(q, 1)]
                shift = (CAP * (s0 + o) - 16 * i).astype(F32)
                parts.append(
                    jnp.where(place[:, None, :] + shift == slot_row, 1.0, 0.0).reshape(DST * 16, TOK)
                )
            pick = jnp.concatenate(parts, axis=1).astype(BF16)
            rows = gt[h, pl.ds(s0, 2)].reshape(2 * TOK, WIDE)
            made = dot(pick, rows).astype(BF16).reshape(DST, 16, WIDE)
            packed[buf, :, pl.ds(pl.multiple_of(16 * i, 16), 16), :] = made
            return carry

        lax.fori_loop(0, TILES, step, 0)

    near_b = [(d, dc) for d in (1, 3, 2, 0) for dc in range(2) if d or dc]

    def scatter(q, h, d, dc):
        buf = units.index((q, h)) % SLOTS
        bb, cc = (b + d) % 4, (c + dc) % 2
        return remote(
            packed.at[buf, bb * 2 + cc], recv.at[q, 2 * d + dc, :, columns(h)],
            a_s.at[q, h, 2 * d + dc], a_r.at[q, h, 2 * d + dc], device(a, y, bb, cc),
        )

    def scatter_own(q, h):
        buf = units.index((q, h)) % SLOTS
        return pltpu.make_async_copy(
            packed.at[buf, b * 2 + c], recv.at[q, 0, :, columns(h)], loc_sem.at[q, h]
        )

    def scatter_sent(q, h):
        for d, dc in near_b:
            scatter(q, h, d, dc).wait_send()
        scatter_own(q, h).wait()

    def pack_and_send(q, h):
        for d in range(4):
            for dy in range(2):
                fetch(q, h, d, dy).wait()
        pack(q, h, units.index((q, h)) % SLOTS)
        for d, dc in near_b:
            scatter(q, h, d, dc).start()
        scatter_own(q, h).start()

    def scatter_wait(q, k):
        for h in range(PARTS):

            @pl.when(k > 0)
            def _():
                scatter(q, h, k, 0).wait_recv()

            scatter(q, h, k, 1).wait_recv()

    def result_same(p, h, k):
        return remote(
            recv.at[p, 2 * k, :, columns(h)], back.at[p, b * 2 + c, :, columns(h)],
            o_s.at[p, h, 2 * k], o_r.at[p, h, 2 * k], device(a, y, (b - k + 4) % 4, c),
        )

    def result_other(p, h, k):
        return remote(
            recv.at[p, 2 * k + 1, :, columns(h)], back.at[p, a * 2 + c, :, columns(h)],
            o_s.at[p, h, 2 * k + 1], o_r.at[p, h, 2 * k + 1], device((a - k + 4) % 4, y, b, 1 - c),
        )

    def result_own(p, h):
        return pltpu.make_async_copy(
            recv.at[p, 0, :, columns(h)], back.at[p, b * 2 + c, :, columns(h)], oloc_sem.at[p, h]
        )

    def send_results(p, h, k):
        @pl.when(k == 0)
        def _():
            result_own(p, h).start()

        @pl.when(k > 0)
        def _():
            result_same(p, h, k).start()

        result_other(p, h, k).start()

    def results_wait(p, h):
        result_own(p, h).wait()
        for k in range(4):
            if k:
                result_same(p, h, k).wait_recv()
            result_other(p, h, k).wait_recv()

    def results_sent(p, h):
        for k in range(4):
            if k:
                result_same(p, h, k).wait_send()
            result_other(p, h, k).wait_send()

    def forward_hidden(k):
        scatter_wait(0, k)
        rows = recv[0, pl.ds(2 * k, 2)].reshape(2 * BLK, 2048)
        for n in range(3):
            cols = slice(256 * n, 256 * n + 256)
            gate = dot(rows, wg[:, cols])
            up = dot(rows, wu[:, cols])
            hid[0, k, :, cols] = (gate * jax.nn.sigmoid(gate) * up).astype(BF16)

    def forward_part(h, k):
        for n in range(WIDE // 512):
            cols = slice(WIDE * h + 512 * n, WIDE * h + 512 * n + 512)
            recv[0, pl.ds(2 * k, 2), :, cols] = (
                dot(hid[0, k], wd[:, cols]).astype(BF16).reshape(2, BLK, 512)
            )
        send_results(0, h, k)

    def backward_hidden(k):
        scatter_wait(1, k)
        scatter_wait(2, k)
        rows = recv[1, pl.ds(2 * k, 2)].reshape(2 * BLK, 2048)
        cot = recv[2, pl.ds(2 * k, 2)].reshape(2 * BLK, 2048)
        for n in range(3):
            cols = slice(256 * n, 256 * n + 256)
            gate = dot(rows, wg[:, cols])
            up = dot(rows, wu[:, cols])
            grad = dot_nt(cot, wd[cols, :])
            sig = jax.nn.sigmoid(gate)
            hid[0, k, :, cols] = (grad * up * sig * (1.0 + gate * (1.0 - sig))).astype(BF16)
            hid[1, k, :, cols] = (grad * gate * sig).astype(BF16)

    def backward_part(h, k):
        for n in range(WIDE // 512):
            cols = slice(WIDE * h + 512 * n, WIDE * h + 512 * n + 512)
            recv[1, pl.ds(2 * k, 2), :, cols] = (
                (dot_nt(hid[0, k], wg[cols, :]) + dot_nt(hid[1, k], wu[cols, :]))
                .astype(BF16)
                .reshape(2, BLK, 512)
            )
        send_results(1, h, k)

    def loop(*steps):
        def body(k, carry):
            for step in steps:
                step(k)
            return carry

        lax.fori_loop(0, 4, body, 0)

    pair_row = lax.broadcasted_iota(jnp.int32, (DST, 32, TOK), 1).astype(F32)

    def partial(p, h, d, dy):
        s = source(d, dy)
        place = table[s, 2 * p]
        weight = table[s, 2 * p + 1]
        hit = place[:, None, :] + s.astype(F32) == pair_row
        mix = jnp.where(hit, weight[:, None, :], 0.0).reshape(DST * 32, TOK).astype(BF16)
        rows = back[p, :, pl.ds(pl.multiple_of(16 * s, 16), 32), columns(h)]
        return dot_tn(mix, rows.reshape(DST * 32, WIDE))

    sums = gt

    def c1(p, h, d):
        part = pl.ds(0, REDUCE[p])
        return remote(
            sums.at[h, 2 * d + 1, part], crossed.at[p, d - 1, part, columns(h)],
            c1_s.at[p, h, d], c1_r.at[p, h, d], at_a(d),
        )

    def c2(p, h, d):
        part = pl.ds(REDUCE[p], TOK - REDUCE[p])
        dst = crossed.at[p, d - 1, part, columns(h)] if d else f_y.at[p, part, columns(h)]
        return remote(
            sums.at[h, 2 * d + 1, part], dst, c2_s.at[p, h, d], c2_r.at[p, h, d], at_a(0, 1)
        )

    def c3(p, h):
        part = pl.ds(0, REDUCE[p])
        return remote(
            sums.at[h, 1, part], f_y.at[p, part, columns(h)], c3_s.at[p, h], c3_r.at[p, h],
            at_a(0, 1),
        )

    def c4(p, h, d):
        return remote(
            sums.at[h, 2 * d], f_a.at[p, d - 1, :, columns(h)],
            c4_s.at[p, h, d], c4_r.at[p, h, d], at_a(d),
        )

    def combine_start(p, h):
        cols = columns(h)
        results_wait(p, h)
        for d in (1, 3, 2):
            sums[h, 2 * d + 1] = partial(p, h, d, 1).astype(BF16)
            c1(p, h, d).start()
            c2(p, h, d).start()
        sums[h, 1] = partial(p, h, 0, 1).astype(BF16)
        c2(p, h, 0).start()
        for d in (1, 3, 2):
            sums[h, 2 * d] = partial(p, h, d, 0).astype(BF16)
        acc[:, cols] = partial(p, h, 0, 0) + inputs[2 * p][:, cols].astype(F32)

    def combine_middle(p, h):
        cols = columns(h)
        cut = REDUCE[p]
        for d in (1, 3, 2):
            c2(p, h, d).wait_recv()
            sums[h, 2 * d, cut:, :] = (
                sums[h, 2 * d, cut:, :].astype(F32) + crossed[p, d - 1, cut:, cols].astype(F32)
            ).astype(BF16)
            c4(p, h, d).start()
        for d in (1, 3, 2):
            c1(p, h, d).wait_recv()
        total = sums[h, 1, :cut, :].astype(F32)
        for d in (1, 2, 3):
            total += crossed[p, d - 1, :cut, cols].astype(F32)
        sums[h, 1, :cut, :] = total.astype(BF16)
        c3(p, h).start()

    def hand(p, h):
        part = ready.at[:, columns(h)]
        return remote(part, handed.at[:, columns(h)], h_s.at[p, h], h_r.at[p, h], (1 - seg, me))

    def combine_end(p, h):
        cols = columns(h)
        for d in (1, 3, 2):
            c4(p, h, d).wait_recv()
        c2(p, h, 0).wait_recv()
        c3(p, h).wait_recv()
        total = acc[:, cols] + f_y[p, :, cols].astype(F32)
        for d in (1, 2, 3):
            total += f_a[p, d - 1, :, cols].astype(F32)

        @pl.when(seg == p)
        def _():
            ready[:, cols] = total.astype(BF16)
            hand(p, h).start()

        @pl.when(seg == 1 - p)
        def _():
            finished[:, cols] = total.astype(BF16)

    def combine_sent(p, h):
        for d in range(4):
            if d:
                c1(p, h, d).wait_send()
                c4(p, h, d).wait_send()
            c2(p, h, d).wait_send()
        c3(p, h).wait_send()

    def stage(step, i):
        if i < len(units):
            step(*units[i])

    stage(gather_relay, 0)
    stage(gather_own, 1)
    stage(gather_onward, 0)
    stage(gather_relay, 1)
    stage(gather_own, 2)
    for i, unit in enumerate(units):
        gather_rest(*unit)
        if i == 0:
            for d, dy in near:
                send_table(d, dy).wait_recv()
        if i >= SLOTS:
            scatter_sent(*units[i - SLOTS])
        pack_and_send(*unit)
        stage(gather_onward, i + 1)
        stage(gather_relay, i + 2)
        stage(gather_own, i + 3)
    for load in loads:
        load.wait()
    for unit in units[-SLOTS:]:
        scatter_own(*unit).wait()
    loop(backward_hidden, functools.partial(backward_part, 0))
    for h in range(1, PARTS):
        loop(functools.partial(backward_part, h))
    combine_start(1, 0)
    loop(forward_hidden, functools.partial(forward_part, 0))
    combine_start(1, 1)
    combine_middle(1, 0)
    loop(functools.partial(forward_part, 1))
    combine_middle(1, 1)
    for h in range(PARTS):
        combine_end(1, h)
        combine_sent(1, h)
        combine_start(0, h)
    for h in range(PARTS):
        combine_middle(0, h)
    for h in range(PARTS):
        combine_end(0, h)
    for h in range(PARTS):
        combine_sent(0, h)

    for p in range(2):
        for h in range(PARTS):
            results_sent(p, h)

            @pl.when(seg == p)
            def _():
                hand(p, h).wait_send()

            @pl.when(seg == 1 - p)
            def _():
                hand(p, h).wait_recv()

    for d, dy in near:
        send_table(d, dy).wait_send()
    for q, h in units:
        gather_sent(q, h)
    for q, h in units[-SLOTS:]:
        for d, dc in near_b:
            scatter(q, h, d, dc).wait_send()


def moe(xf, xb, xc, routes, weights, wg, wu, wd):
    vmem = pl.BlockSpec(memory_space=pltpu.VMEM)
    hbm = pl.BlockSpec(memory_space=pl.ANY)
    dma = pltpu.SemaphoreType.DMA
    block = (TOK, 2048)
    finished, handed, _ = pl.pallas_call(
        kernel,
        out_shape=(
            jax.ShapeDtypeStruct(block, BF16),
            jax.ShapeDtypeStruct(block, BF16),
            jax.ShapeDtypeStruct((3, PARTS, SRC, TOK, WIDE), BF16),
        ),
        in_specs=[vmem] * 5 + [hbm] * 3,
        out_specs=(vmem, vmem, hbm),
        scratch_shapes=[
            pltpu.VMEM((8, 4, 8, TOK), F32),
            pltpu.VMEM((8, 4, 8, TOK), F32),
            pltpu.VMEM((PARTS, SRC, TOK, WIDE), BF16),
            pltpu.VMEM((SLOTS, DST, BLK, WIDE), BF16),
            pltpu.VMEM((3, 8, BLK, 2048), BF16),
            pltpu.VMEM((2, DST, BLK, 2048), BF16),
            pltpu.VMEM((2, 3) + block, BF16),
            pltpu.VMEM((2,) + block, BF16),
            pltpu.VMEM((2, 3) + block, BF16),
            pltpu.VMEM(block, F32),
            pltpu.VMEM(block, BF16),
            pltpu.VMEM((2, 4, 2 * BLK, 768), BF16),
            pltpu.VMEM((2048, 768), BF16),
            pltpu.VMEM((2048, 768), BF16),
            pltpu.VMEM((768, 2048), BF16),
            dma((3,)), dma((PARTS, 8)), dma((3, PARTS)), dma((2, PARTS)),
            dma((8,)), dma((8,)),
            dma((3, PARTS)), dma((3, PARTS)),
            dma((3, PARTS, 4)), dma((3, PARTS, 4)),
            dma((3, PARTS, 4)), dma((3, PARTS, 4)),
            dma((3, PARTS, 4)), dma((3, PARTS, 4)),
            dma((3, PARTS, 4)), dma((3, PARTS, 4)),
            dma((3, PARTS, 4)), dma((3, PARTS, 4)),
            dma((3, PARTS, 8)), dma((3, PARTS, 8)),
            dma((2, PARTS, 8)), dma((2, PARTS, 8)),
            dma((2, PARTS, 4)), dma((2, PARTS, 4)),
            dma((2, PARTS, 4)), dma((2, PARTS, 4)),
            dma((2, PARTS)), dma((2, PARTS)),
            dma((2, PARTS, 4)), dma((2, PARTS, 4)),
            dma((2, PARTS)), dma((2, PARTS)),
        ],
        compiler_params=pltpu.CompilerParams(
            collective_id=0, has_side_effects=True, vmem_limit_bytes=63 * 2**20
        ),
    )(xf, xb, xc, routes, weights, wg, wu, wd)
    return finished, handed


def per_device(
    forward_inputs,
    backward_inputs,
    backward_cotangents,
    routes,
    route_weights,
    w_gate,
    w_up,
    w_down,
):
    finished, handed = moe(
        forward_inputs[0],
        backward_inputs[0],
        backward_cotangents[0],
        routes[:, 0].transpose(0, 2, 1),
        route_weights[:, 0].transpose(0, 2, 1),
        w_gate[0, 0],
        w_up[0, 0],
        w_down[0, 0],
    )
    return (finished[None], handed[None])


def solution(mesh):
    placed = (
        P("segment", "expert", None),
        P("segment", "expert", None),
        P("segment", "expert", None),
        P(None, "segment", "expert", None),
        P(None, "segment", "expert", None),
        P("segment", "expert", None, None),
        P("segment", "expert", None, None),
        P("segment", "expert", None, None),
    )
    return jax.shard_map(
        per_device,
        mesh=mesh,
        in_specs=placed,
        out_specs=(P("segment", "expert", None), P("segment", "expert", None)),
        check_vma=False,
    )
```

```python
import functools

import jax
import jax.numpy as jnp
from jax import lax
from jax.experimental import pallas as pl
from jax.experimental.pallas import tpu as pltpu
from jax.sharding import PartitionSpec as P

MESH = pl.DeviceIdType.MESH
F32 = jnp.float32
BF16 = jnp.bfloat16

TOK = 128
CAP = 17
SRC = 8
DST = 8
BLK = 144
TILES = BLK // 16
FAR = (2, 1, 3)
DIRECT = (32, 96, 32)
REDUCE = (96, 16)
PARTS = 2
WIDE = 2048 // PARTS
SLOTS = 4


def dot(left, right):
    return jnp.dot(left, right, preferred_element_type=F32)


def dot_nt(left, right):
    return lax.dot_general(left, right, (((1,), (1,)), ((), ())), preferred_element_type=F32)


def dot_tn(left, right):
    return lax.dot_general(left, right, (((0,), (0,)), ((), ())), preferred_element_type=F32)


def kernel(
    xf, xb, xc, routes, weights, wg_hbm, wu_hbm, wd_hbm,
    finished, handed, gathered,
    town, table, gt, packed, recv, back, crossed, f_y, f_a, acc, ready, hid, wg, wu, wd,
    w_sem, fetch_sem, loc_sem, oloc_sem,
    t_s, t_r, g1_s, g1_r, g2_s, g2_r, g2f_s, g2f_r, g3_s, g3_r, g3f_s, g3f_r, g4_s, g4_r, a_s, a_r, o_s, o_r,
    c1_s, c1_r, c2_s, c2_r, c3_s, c3_r, c4_s, c4_r, h_s, h_r,
):
    seg = lax.axis_index("segment")
    me = lax.axis_index("expert")
    z, y, x, c = me // 16, (me // 8) % 2, (me // 2) % 4, me % 2
    a = z * (1 - c) + x * c
    b = x * (1 - c) + z * c
    inputs = (xf, xb, xc)

    def device(aa, yy, bb, cc):
        zz = aa * (1 - c) + bb * c
        xx = bb * (1 - c) + aa * c
        return (seg, ((zz * 2 + yy) * 4 + xx) * 2 + cc)

    def at_a(d, dy=0):
        return device((a + d) % 4, (y + dy) % 2, b, c)

    def source(d, dy=0):
        return ((a + d + 4) % 4) * 2 + (y + dy) % 2

    own = a * 2 + y

    def remote(src, dst, send, rec, to):
        return pltpu.make_async_remote_copy(
            src_ref=src, dst_ref=dst, send_sem=send, recv_sem=rec, device_id=to, device_id_type=MESH
        )

    loads = [
        pltpu.make_async_copy(src, dst, w_sem.at[i])
        for i, (src, dst) in enumerate(((wg_hbm, wg), (wu_hbm, wu), (wd_hbm, wd)))
    ]

    barrier = pltpu.get_barrier_semaphore()
    partners = [at_a(d, dy) for d in range(4) for dy in range(2) if d or dy]
    partners += [device(a, y, (b + d) % 4, c) for d in (1, 2, 3)]
    partners += [device(a, y, (b + d) % 4, 1 - c) for d in range(4)]
    partners += [device((a + d) % 4, y, b, 1 - c) for d in (1, 2, 3)]
    partners += [(1 - seg, me)]
    for to in partners:
        pl.semaphore_signal(barrier, inc=1, device_id=to, device_id_type=MESH)
    pl.semaphore_wait(barrier, len(partners))

    def columns(h):
        return pl.ds(WIDE * h, WIDE)

    def g1(q, h):
        return remote(
            inputs[q].at[:, columns(h)], gathered.at[q, h, own], g1_s.at[q, h], g1_r.at[q, h], at_a(0, 1)
        )

    def g2(q, h, d):
        return remote(
            inputs[q].at[:, columns(h)], gathered.at[q, h, own], g2_s.at[q, h, d], g2_r.at[q, h, d],
            at_a(d),
        )

    def g2f(q, h, d):
        part = gathered.at[q, h, source(-d), pl.ds(0 if d == 1 else TOK // 2, TOK // 2)]
        return remote(part, part, g2f_s.at[q, h, d], g2f_r.at[q, h, d], at_a(d))

    def g3(q, h, d):
        part = gathered.at[q, h, source(0, 1), pl.ds(0, DIRECT[q])]
        return remote(part, part, g3_s.at[q, h, d], g3_r.at[q, h, d], at_a(d))

    def g3f(q, h, d):
        half = DIRECT[q] // 2
        part = gathered.at[q, h, source(-d, 1), pl.ds(0 if d == 1 else half, half)]
        return remote(part, part, g3f_s.at[q, h, d], g3f_r.at[q, h, d], at_a(d))

    def g4(q, h, d):
        part = gathered.at[q, h, source(-d), pl.ds(DIRECT[q], TOK - DIRECT[q])]
        return remote(part, part, g4_s.at[q, h, d], g4_r.at[q, h, d], at_a(0, 1))

    def fetch(q, h, d, dy):
        s = source(d, dy)
        src = inputs[q].at[:, columns(h)] if (d, dy) == (0, 0) else gathered.at[q, h, s]
        return pltpu.make_async_copy(src, gt.at[h, s], fetch_sem.at[h, 2 * d + dy])

    def gather_own(q, h):
        g1(q, h).start()
        for d in (1, 3):
            g2(q, h, d).start()

    def gather_relay(q, h):
        g1(q, h).wait_recv()
        for d in (1, 3):
            g3(q, h, d).start()
        for d in (1, 3):
            g2(q, h, d).wait_recv()
            g2f(q, h, d).start()
            g4(q, h, d).start()

    def gather_onward(q, h):
        for d in (1, 3):
            g3(q, h, d).wait_recv()
            g3f(q, h, d).start()
        for d in (1, 3):
            g2f(q, h, d).wait_recv()
        g4(q, h, 2).start()
        for dy in range(2):
            fetch(q, h, 0, dy).start()
        for d in range(1, 4):
            fetch(q, h, d, 0).start()

    def gather_rest(q, h):
        for d in (1, 3):
            g4(q, h, d).wait_recv()
            fetch(q, h, 4 - d, 1).start()
        for d in (1, 3):
            g3f(q, h, d).wait_recv()
        g4(q, h, 2).wait_recv()
        fetch(q, h, 2, 1).start()

    def gather_sent(q, h):
        g1(q, h).wait_send()
        for d in (1, 3):
            g2(q, h, d).wait_send()
            g2f(q, h, d).wait_send()
            g3(q, h, d).wait_send()
            g3f(q, h, d).wait_send()
        for d in FAR:
            g4(q, h, d).wait_send()

    units = [(q, h) for q in (1, 2, 0) for h in range(PARTS)]
    gather_own(*units[0])
    for load in loads:
        load.start()

    row = lax.broadcasted_iota(jnp.int32, (64, TOK), 0)
    ra, ry, rb, rc = row // 16, (row // 8) % 2, (row // 2) % 4, row % 2
    expert = (
        ((ra * (1 - c) + rb * c) * 2 + ry) * 4 + (rb * (1 - c) + ra * c)
    ) * 2 + rc
    before = (
        lax.broadcasted_iota(jnp.int32, (TOK, TOK), 0)
        < lax.broadcasted_iota(jnp.int32, (TOK, TOK), 1)
    ).astype(F32).astype(BF16)
    for p in range(2):
        named = jnp.zeros((64, TOK), F32)
        weight = jnp.zeros((64, TOK), F32)
        for j in range(8):
            hit = routes[p, j : j + 1, :] == expert
            named = jnp.where(hit, 1.0, named)
            weight = jnp.where(hit, weights[p, j : j + 1, :], weight)
        prior = dot(named.astype(BF16), before)
        place = jnp.where(named > 0.5, prior, -1000.0)
        for g in range(8):
            town[g, 2 * p] = place[8 * g : 8 * g + 8]
            town[g, 2 * p + 1] = weight[8 * g : 8 * g + 8]

    def send_table(d, dy):
        return remote(
            town.at[source(d, dy)], table.at[own], t_s.at[2 * d + dy], t_r.at[2 * d + dy], at_a(d, dy)
        )

    near = [(d, dy) for d in range(4) for dy in range(2) if d or dy]
    for d, dy in near:
        send_table(d, dy).start()
    table[own] = town[own]

    slot_row = lax.broadcasted_iota(jnp.int32, (DST, 16, TOK), 1).astype(F32)

    def pack(q, h, buf):
        def step(i, carry):
            s0 = jnp.clip(i - 1, 0, SRC - 2)
            parts = []
            for o in range(2):
                place = table[s0 + o, 2 * min(q, 1)]
                shift = (CAP * (s0 + o) - 16 * i).astype(F32)
                parts.append(
                    jnp.where(place[:, None, :] + shift == slot_row, 1.0, 0.0).reshape(DST * 16, TOK)
                )
            pick = jnp.concatenate(parts, axis=1).astype(BF16)
            rows = gt[h, pl.ds(s0, 2)].reshape(2 * TOK, WIDE)
            made = dot(pick, rows).astype(BF16).reshape(DST, 16, WIDE)
            packed[buf, :, pl.ds(pl.multiple_of(16 * i, 16), 16), :] = made
            return carry

        lax.fori_loop(0, TILES, step, 0)

    near_b = [(d, dc) for d in (0, 1, 3, 2) for dc in range(2) if d or dc]

    def scatter(q, h, d, dc):
        buf = units.index((q, h)) % SLOTS
        bb, cc = (b + d) % 4, (c + dc) % 2
        return remote(
            packed.at[buf, bb * 2 + cc], recv.at[q, 2 * d + dc, :, columns(h)],
            a_s.at[q, h, 2 * d + dc], a_r.at[q, h, 2 * d + dc], device(a, y, bb, cc),
        )

    def scatter_own(q, h):
        buf = units.index((q, h)) % SLOTS
        return pltpu.make_async_copy(
            packed.at[buf, b * 2 + c], recv.at[q, 0, :, columns(h)], loc_sem.at[q, h]
        )

    def scatter_sent(q, h):
        for d, dc in near_b:
            scatter(q, h, d, dc).wait_send()
        scatter_own(q, h).wait()

    def pack_and_send(q, h):
        for d in range(4):
            for dy in range(2):
                fetch(q, h, d, dy).wait()
        pack(q, h, units.index((q, h)) % SLOTS)
        for d, dc in near_b:
            scatter(q, h, d, dc).start()
        scatter_own(q, h).start()

    def scatter_wait(q, k):
        for h in range(PARTS):

            @pl.when(k > 0)
            def _():
                scatter(q, h, k, 0).wait_recv()

            scatter(q, h, k, 1).wait_recv()

    def result_same(p, h, k):
        return remote(
            recv.at[p, 2 * k, :, columns(h)], back.at[p, b * 2 + c, :, columns(h)],
            o_s.at[p, h, 2 * k], o_r.at[p, h, 2 * k], device(a, y, (b - k + 4) % 4, c),
        )

    def result_other(p, h, k):
        return remote(
            recv.at[p, 2 * k + 1, :, columns(h)], back.at[p, a * 2 + c, :, columns(h)],
            o_s.at[p, h, 2 * k + 1], o_r.at[p, h, 2 * k + 1], device((a - k + 4) % 4, y, b, 1 - c),
        )

    def result_own(p, h):
        return pltpu.make_async_copy(
            recv.at[p, 0, :, columns(h)], back.at[p, b * 2 + c, :, columns(h)], oloc_sem.at[p, h]
        )

    def send_results(p, h, k):
        @pl.when(k == 0)
        def _():
            result_own(p, h).start()

        @pl.when(k > 0)
        def _():
            result_same(p, h, k).start()

        result_other(p, h, k).start()

    def results_wait(p, h):
        result_own(p, h).wait()
        for k in range(4):
            if k:
                result_same(p, h, k).wait_recv()
            result_other(p, h, k).wait_recv()

    def results_sent(p, h):
        for k in range(4):
            if k:
                result_same(p, h, k).wait_send()
            result_other(p, h, k).wait_send()

    def forward_hidden(k):
        scatter_wait(0, k)
        rows = recv[0, pl.ds(2 * k, 2)].reshape(2 * BLK, 2048)
        for n in range(3):
            cols = slice(256 * n, 256 * n + 256)
            gate = dot(rows, wg[:, cols])
            up = dot(rows, wu[:, cols])
            hid[0, k, :, cols] = (gate * jax.nn.sigmoid(gate) * up).astype(BF16)

    def forward_part(h, k):
        for n in range(WIDE // 512):
            cols = slice(WIDE * h + 512 * n, WIDE * h + 512 * n + 512)
            recv[0, pl.ds(2 * k, 2), :, cols] = (
                dot(hid[0, k], wd[:, cols]).astype(BF16).reshape(2, BLK, 512)
            )
        send_results(0, h, k)

    def backward_hidden(k):
        scatter_wait(1, k)
        scatter_wait(2, k)
        rows = recv[1, pl.ds(2 * k, 2)].reshape(2 * BLK, 2048)
        cot = recv[2, pl.ds(2 * k, 2)].reshape(2 * BLK, 2048)
        for n in range(3):
            cols = slice(256 * n, 256 * n + 256)
            gate = dot(rows, wg[:, cols])
            up = dot(rows, wu[:, cols])
            grad = dot_nt(cot, wd[cols, :])
            sig = jax.nn.sigmoid(gate)
            hid[0, k, :, cols] = (grad * up * sig * (1.0 + gate * (1.0 - sig))).astype(BF16)
            hid[1, k, :, cols] = (grad * gate * sig).astype(BF16)

    def backward_part(h, k):
        for n in range(WIDE // 512):
            cols = slice(WIDE * h + 512 * n, WIDE * h + 512 * n + 512)
            recv[1, pl.ds(2 * k, 2), :, cols] = (
                (dot_nt(hid[0, k], wg[cols, :]) + dot_nt(hid[1, k], wu[cols, :]))
                .astype(BF16)
                .reshape(2, BLK, 512)
            )
        send_results(1, h, k)

    def loop(*steps):
        def body(k, carry):
            for step in steps:
                step(k)
            return carry

        lax.fori_loop(0, 4, body, 0)

    pair_row = lax.broadcasted_iota(jnp.int32, (DST, 32, TOK), 1).astype(F32)

    def partial(p, h, d, dy):
        s = source(d, dy)
        place = table[s, 2 * p]
        weight = table[s, 2 * p + 1]
        hit = place[:, None, :] + s.astype(F32) == pair_row
        mix = jnp.where(hit, weight[:, None, :], 0.0).reshape(DST * 32, TOK).astype(BF16)
        rows = back[p, :, pl.ds(pl.multiple_of(16 * s, 16), 32), columns(h)]
        return dot_tn(mix, rows.reshape(DST * 32, WIDE))

    sums = gt

    def c1(p, h, d):
        part = pl.ds(0, REDUCE[p])
        return remote(
            sums.at[h, 2 * d + 1, part], crossed.at[p, d - 1, part, columns(h)],
            c1_s.at[p, h, d], c1_r.at[p, h, d], at_a(d),
        )

    def c2(p, h, d):
        part = pl.ds(REDUCE[p], TOK - REDUCE[p])
        dst = crossed.at[p, d - 1, part, columns(h)] if d else f_y.at[p, part, columns(h)]
        return remote(
            sums.at[h, 2 * d + 1, part], dst, c2_s.at[p, h, d], c2_r.at[p, h, d], at_a(0, 1)
        )

    def c3(p, h):
        part = pl.ds(0, REDUCE[p])
        return remote(
            sums.at[h, 1, part], f_y.at[p, part, columns(h)], c3_s.at[p, h], c3_r.at[p, h],
            at_a(0, 1),
        )

    def c4(p, h, d):
        return remote(
            sums.at[h, 2 * d], f_a.at[p, d - 1, :, columns(h)],
            c4_s.at[p, h, d], c4_r.at[p, h, d], at_a(d),
        )

    def combine_start(p, h):
        cols = columns(h)
        results_wait(p, h)
        for d in (1, 3, 2):
            sums[h, 2 * d + 1] = partial(p, h, d, 1).astype(BF16)
            c1(p, h, d).start()
            c2(p, h, d).start()
        sums[h, 1] = partial(p, h, 0, 1).astype(BF16)
        c2(p, h, 0).start()
        for d in (1, 3, 2):
            sums[h, 2 * d] = partial(p, h, d, 0).astype(BF16)
        acc[:, cols] = partial(p, h, 0, 0) + inputs[2 * p][:, cols].astype(F32)

    def combine_middle(p, h):
        cols = columns(h)
        cut = REDUCE[p]
        for d in (1, 3, 2):
            c2(p, h, d).wait_recv()
            sums[h, 2 * d, cut:, :] = (
                sums[h, 2 * d, cut:, :].astype(F32) + crossed[p, d - 1, cut:, cols].astype(F32)
            ).astype(BF16)
            c4(p, h, d).start()
        for d in (1, 3, 2):
            c1(p, h, d).wait_recv()
        total = sums[h, 1, :cut, :].astype(F32)
        for d in (1, 2, 3):
            total += crossed[p, d - 1, :cut, cols].astype(F32)
        sums[h, 1, :cut, :] = total.astype(BF16)
        c3(p, h).start()

    def hand(p, h):
        part = ready.at[:, columns(h)]
        return remote(part, handed.at[:, columns(h)], h_s.at[p, h], h_r.at[p, h], (1 - seg, me))

    def combine_end(p, h):
        cols = columns(h)
        for d in (1, 3, 2):
            c4(p, h, d).wait_recv()
        c2(p, h, 0).wait_recv()
        c3(p, h).wait_recv()
        total = acc[:, cols] + f_y[p, :, cols].astype(F32)
        for d in (1, 2, 3):
            total += f_a[p, d - 1, :, cols].astype(F32)

        @pl.when(seg == p)
        def _():
            ready[:, cols] = total.astype(BF16)
            hand(p, h).start()

        @pl.when(seg == 1 - p)
        def _():
            finished[:, cols] = total.astype(BF16)

    def combine_sent(p, h):
        for d in range(4):
            if d:
                c1(p, h, d).wait_send()
                c4(p, h, d).wait_send()
            c2(p, h, d).wait_send()
        c3(p, h).wait_send()

    def stage(step, i):
        if i < len(units):
            step(*units[i])

    stage(gather_relay, 0)
    stage(gather_own, 1)
    stage(gather_onward, 0)
    stage(gather_relay, 1)
    stage(gather_own, 2)
    for i, unit in enumerate(units):
        gather_rest(*unit)
        if i == 0:
            for d, dy in near:
                send_table(d, dy).wait_recv()
        if i >= SLOTS:
            scatter_sent(*units[i - SLOTS])
        pack_and_send(*unit)
        stage(gather_onward, i + 1)
        stage(gather_relay, i + 2)
        stage(gather_own, i + 3)
    for load in loads:
        load.wait()
    for unit in units[-SLOTS:]:
        scatter_own(*unit).wait()
    loop(backward_hidden, functools.partial(backward_part, 0))
    for h in range(1, PARTS):
        loop(functools.partial(backward_part, h))
    combine_start(1, 0)
    loop(forward_hidden, functools.partial(forward_part, 0))
    combine_start(1, 1)
    combine_middle(1, 0)
    loop(functools.partial(forward_part, 1))
    combine_middle(1, 1)
    for h in range(PARTS):
        combine_end(1, h)
        combine_sent(1, h)
        combine_start(0, h)
    for h in range(PARTS):
        combine_middle(0, h)
    for h in range(PARTS):
        combine_end(0, h)
    for h in range(PARTS):
        combine_sent(0, h)

    for p in range(2):
        for h in range(PARTS):
            results_sent(p, h)

            @pl.when(seg == p)
            def _():
                hand(p, h).wait_send()

            @pl.when(seg == 1 - p)
            def _():
                hand(p, h).wait_recv()

    for d, dy in near:
        send_table(d, dy).wait_send()
    for q, h in units:
        gather_sent(q, h)
    for q, h in units[-SLOTS:]:
        for d, dc in near_b:
            scatter(q, h, d, dc).wait_send()


def moe(xf, xb, xc, routes, weights, wg, wu, wd):
    vmem = pl.BlockSpec(memory_space=pltpu.VMEM)
    hbm = pl.BlockSpec(memory_space=pl.ANY)
    dma = pltpu.SemaphoreType.DMA
    block = (TOK, 2048)
    finished, handed, _ = pl.pallas_call(
        kernel,
        out_shape=(
            jax.ShapeDtypeStruct(block, BF16),
            jax.ShapeDtypeStruct(block, BF16),
            jax.ShapeDtypeStruct((3, PARTS, SRC, TOK, WIDE), BF16),
        ),
        in_specs=[vmem] * 5 + [hbm] * 3,
        out_specs=(vmem, vmem, hbm),
        scratch_shapes=[
            pltpu.VMEM((8, 4, 8, TOK), F32),
            pltpu.VMEM((8, 4, 8, TOK), F32),
            pltpu.VMEM((PARTS, SRC, TOK, WIDE), BF16),
            pltpu.VMEM((SLOTS, DST, BLK, WIDE), BF16),
            pltpu.VMEM((3, 8, BLK, 2048), BF16),
            pltpu.VMEM((2, DST, BLK, 2048), BF16),
            pltpu.VMEM((2, 3) + block, BF16),
            pltpu.VMEM((2,) + block, BF16),
            pltpu.VMEM((2, 3) + block, BF16),
            pltpu.VMEM(block, F32),
            pltpu.VMEM(block, BF16),
            pltpu.VMEM((2, 4, 2 * BLK, 768), BF16),
            pltpu.VMEM((2048, 768), BF16),
            pltpu.VMEM((2048, 768), BF16),
            pltpu.VMEM((768, 2048), BF16),
            dma((3,)), dma((PARTS, 8)), dma((3, PARTS)), dma((2, PARTS)),
            dma((8,)), dma((8,)),
            dma((3, PARTS)), dma((3, PARTS)),
            dma((3, PARTS, 4)), dma((3, PARTS, 4)),
            dma((3, PARTS, 4)), dma((3, PARTS, 4)),
            dma((3, PARTS, 4)), dma((3, PARTS, 4)),
            dma((3, PARTS, 4)), dma((3, PARTS, 4)),
            dma((3, PARTS, 4)), dma((3, PARTS, 4)),
            dma((3, PARTS, 8)), dma((3, PARTS, 8)),
            dma((2, PARTS, 8)), dma((2, PARTS, 8)),
            dma((2, PARTS, 4)), dma((2, PARTS, 4)),
            dma((2, PARTS, 4)), dma((2, PARTS, 4)),
            dma((2, PARTS)), dma((2, PARTS)),
            dma((2, PARTS, 4)), dma((2, PARTS, 4)),
            dma((2, PARTS)), dma((2, PARTS)),
        ],
        compiler_params=pltpu.CompilerParams(
            collective_id=0, has_side_effects=True, vmem_limit_bytes=63 * 2**20
        ),
    )(xf, xb, xc, routes, weights, wg, wu, wd)
    return finished, handed


def per_device(
    forward_inputs,
    backward_inputs,
    backward_cotangents,
    routes,
    route_weights,
    w_gate,
    w_up,
    w_down,
):
    finished, handed = moe(
        forward_inputs[0],
        backward_inputs[0],
        backward_cotangents[0],
        routes[:, 0].transpose(0, 2, 1),
        route_weights[:, 0].transpose(0, 2, 1),
        w_gate[0, 0],
        w_up[0, 0],
        w_down[0, 0],
    )
    return (finished[None], handed[None])


def solution(mesh):
    placed = (
        P("segment", "expert", None),
        P("segment", "expert", None),
        P("segment", "expert", None),
        P(None, "segment", "expert", None),
        P(None, "segment", "expert", None),
        P("segment", "expert", None, None),
        P("segment", "expert", None, None),
        P("segment", "expert", None, None),
    )
    return jax.shard_map(
        per_device,
        mesh=mesh,
        in_specs=placed,
        out_specs=(P("segment", "expert", None), P("segment", "expert", None)),
        check_vma=False,
    )
```
